128 devices in a mesh: roll: 8 (over x_lo, y), head: 16 (over x_hi, z, core).
Axes of the slice: x: 4 (x_hi: 2, x_lo: 2; x = x_hi * 2 + x_lo), y: 4, z: 4, core: 2. Of those that a mesh axis runs over, the one named last changes fastest.
Arguments:
- queries: bfloat16 [16, 1024, 8192], P('roll', None, 'head'), may hold values from -0.5 to 0.5
- keys: bfloat16 [16, 1024, 8192], P('roll', None, 'head'), may hold values from -0.5 to 0.5
- values: bfloat16 [16, 1024, 8192], P('roll', None, 'head'), may hold values from -6 to 6
- out_grad: bfloat16 [16, 1024, 8192], P('roll', None, 'head'), may hold values from -6 to 6
- prompt_keys: bfloat16 [8, 1024, 8192], P('roll', None, 'head'), may hold values from -0.5 to 0.5
- prompt_values: bfloat16 [8, 1024, 8192], P('roll', None, 'head'), may hold values from -6 to 6
- rollout_prompt: int32 [16], P('roll'), may hold values from 0 to 7
- roll_lengths: int32 [16], P('roll'), may hold values from 128 to 1024, as said below
- decay_exp: int32 [64], P('head'), may hold values from 5 to 14
- gain: bfloat16 [8192], P('head'), may hold values from 0.099609375 to 1.8984375
Outputs:
- normed: bfloat16 [16, 1024, 8192], P('roll', None, 'head')
- query_grad: bfloat16 [16, 1024, 8192], P('roll', None, 'head')
- key_grad: bfloat16 [16, 1024, 8192], P('roll', None, 'head')
- value_grad: bfloat16 [16, 1024, 8192], P('roll', None, 'head')
- prompt_key_grad: bfloat16 [8, 1024, 8192], P('roll', None, 'head')
- prompt_value_grad: bfloat16 [8, 1024, 8192], P('roll', None, 'head')
The draws below stay inside these ranges and needn't reach their ends.
Inputs may be any that keep to these rules, and one draw needn't show every extreme that they name: `roll_lengths`: some rollout in every draw has all 1024 slots live.
All inputs are finite; a program needn't handle non-finite values.
Results may differ from the reference program's by a relative error of at most 0.0011.
Values sent between devices are 32-bit elements; how exact they have to be, the bound alone decides.
A program may use at most 192 MiB of HBM per device.

```python
import jax
import jax.numpy as jnp
from jax import lax

HEADS = 64
DH = 128
LEN = 1024
PLEN = 1024
ROLLS = 16
PROMPTS = 8


def draw_roll_lengths(key, part):
    key = jax.random.fold_in(key, 11)
    first, second = jax.random.split(key)
    sizes = jax.random.randint(first, (ROLLS,), LEN // 8, LEN + 1)
    where = jax.random.randint(second, (), 0, ROLLS)
    return sizes.at[where].set(LEN).astype(jnp.int32)


def set_ends(entries, key, low, largest):
    longest = entries.shape.index(max(entries.shape))
    spots = []
    for shift in (0, 1):
        where = [jax.random.randint(jax.random.fold_in(key, axis), (), 0, length) for axis, length in enumerate(entries.shape)]
        where[longest] = (where[longest] + shift) % entries.shape[longest]
        spots.append(tuple(where))
    return entries.at[spots[0]].set(low).at[spots[1]].set(largest)


def shard_levels(own_key, dims, cuts, low, largest):
    level = 1.0
    for axis_at, blocks in cuts:
        heights = jax.random.uniform(jax.random.fold_in(jax.random.fold_in(own_key, 6), axis_at), (blocks,), jnp.float32, low / len(cuts), largest / len(cuts))
        level = level * jnp.repeat(jnp.exp(heights), dims[axis_at] // blocks).reshape((-1,) + (1,) * (len(dims) - 1 - axis_at))
    return level


def noise(own_key, shape, deviation, most, shards=(), kind=jnp.bfloat16):
    loudness = shard_levels(own_key, shape, shards, -0.22, 0.18) if shards else 1.0
    result = jax.random.normal(own_key, shape, jnp.float32) * deviation * loudness
    return jnp.minimum(jnp.maximum(result, -most), most).astype(kind)


def setup_inputs(seed: int = 0) -> dict:
    seeds = jax.random.split(jax.random.key(seed), 11)
    queries = noise(seeds[0], (ROLLS, LEN, HEADS * DH), DH ** -0.5, 0.5, ((0, 8), (2, 16)))
    keys = noise(seeds[1], (ROLLS, LEN, HEADS * DH), DH ** -0.5, 0.5, ((0, 8), (2, 16)))
    values = noise(seeds[2], (ROLLS, LEN, HEADS * DH), 1.0, 6.0, ((0, 8), (2, 16)))
    out_grad = noise(seeds[3], (ROLLS, LEN, HEADS * DH), 1.0, 6.0, ((0, 8), (2, 16)))
    prompt_keys = noise(seeds[4], (PROMPTS, PLEN, HEADS * DH), DH ** -0.5, 0.5, ((0, 8), (2, 16)))
    prompt_values = noise(seeds[5], (PROMPTS, PLEN, HEADS * DH), 1.0, 6.0, ((0, 8), (2, 16)))
    rollout_prompt = set_ends(jax.random.randint(seeds[6], (ROLLS,), 0, PROMPTS), jax.random.fold_in(seeds[6], 1), 0, PROMPTS - 1).astype(jnp.int32)
    roll_lengths = draw_roll_lengths(jax.random.fold_in(seeds[10], 71), 0)
    decay_exp = set_ends(jax.random.randint(seeds[8], (HEADS,), 5, 15), jax.random.fold_in(seeds[8], 1), 5, 14).astype(jnp.int32)
    gain = jnp.clip(1.0 + 0.18 * jax.random.normal(seeds[9], (HEADS * DH,), jnp.float32), 0.099609375, 1.8984375).astype(jnp.bfloat16)
    return {"queries": queries, "keys": keys, "values": values, "out_grad": out_grad, "prompt_keys": prompt_keys, "prompt_values": prompt_values, "rollout_prompt": rollout_prompt, "roll_lengths": roll_lengths, "decay_exp": decay_exp, "gain": gain}


HI = lax.Precision.HIGHEST
EPS = 1e-06

def block_of(count):
    return 256 if count % 256 == 0 else count

def decay_rates(decay_exp, total):
    return jnp.exp2(-decay_exp.astype(jnp.float32)) * (2048.0 / total)

def tables(rate, block):
    pos = jnp.arange(block).astype(jnp.float32)
    gap = pos[:, None] - pos[None, :]
    intra = jnp.where(gap >= 0.0, jnp.exp(-rate[:, None, None] * jnp.maximum(gap, 0.0)[None]), 0.0)
    qdecay = jnp.exp(-rate[None, :] * (pos[:, None] + 1.0))
    kdecay = jnp.exp(-rate[None, :] * (block - 1.0 - pos[:, None]))
    bdecay = jnp.exp(-rate * block)
    return (intra, qdecay, kdecay, bdecay)

def attend(query, key, value, start, rate):
    length, heads, width = query.shape
    block = block_of(length)
    count = length // block
    intra, qdecay, kdecay, bdecay = tables(rate, block)

    def step(state, pieces):
        qc, kc, vc = pieces
        scores = jnp.einsum('ihd,jhd->hij', qc, kc, precision=HI) * intra
        out = jnp.einsum('hij,jhe->ihe', scores, vc, precision=HI)
        out = out + jnp.einsum('ihd,hde->ihe', qc, state, precision=HI) * qdecay[:, :, None]
        state = state * bdecay[:, None, None] + jnp.einsum('jhd,jhe->hde', kc * kdecay[:, :, None], vc, precision=HI)
        return (state, out)
    split = lambda arr: arr.reshape(count, block, heads, width)
    final, outs = lax.scan(step, start, (split(query), split(key), split(value)))
    return outs.reshape(length, heads, width)

def prompt_state(key, value, rate):
    length, heads, width = key.shape
    block = block_of(length)
    count = length // block
    intra, qdecay, kdecay, bdecay = tables(rate, block)

    def step(state, pieces):
        kc, vc = pieces
        return (state * bdecay[:, None, None] + jnp.einsum('jhd,jhe->hde', kc * kdecay[:, :, None], vc, precision=HI), None)
    split = lambda arr: arr.reshape(count, block, heads, width)
    final, unused = lax.scan(step, jnp.zeros((heads, width, width), jnp.float32), (split(key), split(value)))
    return final

def reference(queries, keys, values, out_grad, prompt_keys, prompt_values, rollout_prompt, roll_lengths, decay_exp, gain):
    rate = decay_rates(decay_exp, PLEN + LEN)
    features = HEADS * DH
    shape_p = (PLEN, HEADS, DH)
    shape_r = (LEN, HEADS, DH)
    gainf = gain.astype(jnp.float32).reshape(HEADS, DH)

    def one_prompt(pair):
        return prompt_state(pair[0].astype(jnp.float32).reshape(shape_p), pair[1].astype(jnp.float32).reshape(shape_p), rate)
    states = lax.map(one_prompt, (prompt_keys, prompt_values))

    def one_rollout(items):
        qr, kr, vr, dy, which, size = items
        start = states[which]
        live = (jnp.arange(LEN) < size).astype(jnp.float32)[:, None, None]

        def forward(a, b, c, s):
            return attend(a, b, c, s, rate) * live
        attn, pull = jax.vjp(forward, qr.astype(jnp.float32).reshape(shape_r), kr.astype(jnp.float32).reshape(shape_r), vr.astype(jnp.float32).reshape(shape_r), start)
        ss = lax.optimization_barrier(jnp.sum(attn * attn, axis=(1, 2)))
        scale = lax.rsqrt(ss / features + EPS)[:, None, None]
        normed = (attn * scale * gainf).astype(jnp.bfloat16).reshape(LEN, features)
        dyg = dy.astype(jnp.float32).reshape(shape_r) * gainf
        cross = lax.optimization_barrier(jnp.sum(dyg * attn, axis=(1, 2)))[:, None, None]
        attn_grad = scale * dyg - attn * scale ** 3 * cross / features
        gq, gk, gv, gs = pull(attn_grad)
        cast = lambda arr: arr.astype(jnp.bfloat16).reshape(LEN, features)
        return (normed, cast(gq), cast(gk), cast(gv), gs)
    normed, query_grad, key_grad, value_grad, start_grad = lax.map(one_rollout, (queries, keys, values, out_grad, rollout_prompt, roll_lengths))
    pick = (rollout_prompt[:, None] == jnp.arange(PROMPTS)[None, :]).astype(jnp.float32)
    state_grad = jnp.einsum('rp,rhde->phde', pick, start_grad, precision=HI)

    def prompt_back(items):
        kp, vp, grad = items
        unused, pull = jax.vjp(lambda a, b: prompt_state(a, b, rate), kp.astype(jnp.float32).reshape(shape_p), vp.astype(jnp.float32).reshape(shape_p))
        gk, gv = pull(grad)
        return (gk.astype(jnp.bfloat16).reshape(PLEN, features), gv.astype(jnp.bfloat16).reshape(PLEN, features))
    prompt_key_grad, prompt_value_grad = lax.map(prompt_back, (prompt_keys, prompt_values, state_grad))
    return (normed, query_grad, key_grad, value_grad, prompt_key_grad, prompt_value_grad)
```

```python
import functools

import jax
import jax.numpy as jnp
from jax import lax
from jax.experimental import pallas as pl
from jax.experimental.pallas import tpu as pltpu
from jax.sharding import PartitionSpec as P

F32 = jnp.float32
BF16 = jnp.bfloat16
EPS = 1e-06
D = 128
C = 128


def nn(a, b):
    return lax.dot_general(a, b, (((1,), (0,)), ((), ())), preferred_element_type=F32)


def nt(a, b):
    return lax.dot_general(a, b, (((1,), (1,)), ((), ())), preferred_element_type=F32)


def lanes(a, b):
    return jnp.concatenate([a, b], axis=1)


def rows(a, b):
    return jnp.concatenate([a, b], axis=0)


def split(x):
    hi = x.astype(BF16)
    return hi, (x - hi.astype(F32)).astype(BF16)


def wide(x):
    return lanes(*split(x))


def tall(x):
    return rows(*split(x))


def rate_of(exponent, shape):
    return jnp.exp2(-jnp.full(shape, exponent, jnp.int32).astype(F32))


def tables(exponent):
    rate = rate_of(exponent, (C, C))
    i = lax.broadcasted_iota(jnp.int32, (C, C), 0).astype(F32)
    j = lax.broadcasted_iota(jnp.int32, (C, C), 1).astype(F32)
    gap = i - j
    decay = jnp.exp(-rate * jnp.abs(gap))
    low = jnp.where(gap >= 0.0, decay, 0.0)
    up = jnp.where(gap <= 0.0, decay, 0.0)
    qd = jnp.exp(-rate * (i + 1.0))
    kd = jnp.exp(-rate * (C - 1.0 - i))
    return low, up, qd, kd


def power(exponent, tokens):
    return jnp.exp(-rate_of(exponent, (1, D)) * float(tokens))


def cut(n):
    return pl.ds(n * C, C)


def state_of_prompt(kp, vp, kd, exponent):
    count = kp.shape[0] // C
    total = None
    for n in range(count):
        vd = vp[cut(n), :].astype(F32) * (kd * power(exponent, C * (count - 1 - n)))
        kt = kp[cut(n), :].T
        part = nn(lanes(kt, kt), tall(vd))
        total = part if total is None else total + part
    return total


def prompt_grads(kp, vp, grad, kd, exponent, gk_ref, gv_ref):
    count = kp.shape[0] // C
    flat, high = wide(grad), tall(grad)
    for n in range(count):
        decay = kd * power(exponent, C * (count - 1 - n))
        k, v = kp[cut(n), :], vp[cut(n), :]
        gk_ref[cut(n), :] = (nt(lanes(v, v), flat) * decay).astype(BF16)
        gv_ref[cut(n), :] = (nn(lanes(k, k), high) * decay).astype(BF16)


def forward_local(q_ref, k_ref, v_ref, tab, exponent, out_ref, state_ref):
    low, up, qd, kd = tab
    step = power(exponent, C)
    state = None
    for n in range(q_ref.shape[0] // C):
        q, k, v = q_ref[cut(n), :], k_ref[cut(n), :], v_ref[cut(n), :]
        out = nn(wide(nt(q, k) * low), rows(v, v))
        kt = k.T
        part = nn(lanes(kt, kt), tall(v.astype(F32) * kd))
        if n == 0:
            state_ref[n] = jnp.zeros((D, D), F32)
            state = part
        else:
            state_ref[n] = state
            out = out + qd * nn(lanes(q, q), tall(state))
            state = state * step + part
        out_ref[cut(n), :] = out


def forward_start(q_ref, g_ref, out_ref, state_ref, start, gain, size, tab, exponent, attn_ref, full_ref, sq_ref, cr_ref, first):
    low, up, qd, kd = tab
    high = tall(start)
    for n in range(q_ref.shape[0] // C):
        q = q_ref[cut(n), :]
        token = lax.broadcasted_iota(jnp.int32, (C, D), 0) + n * C
        lift = power(exponent, C * n)
        attn = out_ref[cut(n), :] + nn(lanes(q, q), high) * (qd * lift)
        attn = jnp.where(token < size, attn, 0.0)
        attn_ref[cut(n), :] = attn
        full_ref[n] = state_ref[n] + start * lift
        dyg = g_ref[cut(n), :].astype(F32) * gain
        square, cross = attn * attn, dyg * attn
        sq_ref[cut(n), :] = jnp.where(first, 0.0, sq_ref[cut(n), :]) + square
        cr_ref[cut(n), :] = jnp.where(first, 0.0, cr_ref[cut(n), :]) + cross


def row_sums(x):
    return nt(jnp.ones((8, 2 * D), BF16), wide(x))


def column(row):
    i = lax.broadcasted_iota(jnp.int32, (C, C), 0)
    j = lax.broadcasted_iota(jnp.int32, (C, C), 1)
    spread = jnp.where(i == j, row, 0.0)
    return nn(wide(spread), jnp.ones((2 * C, D), BF16))


def start_back(q_ref, g_ref, attn_ref, s_ref, c_ref, gain, tab, exponent, normed_ref, hi_ref, lo_ref, grad_ref):
    low, up, qd, kd = tab
    step = power(exponent, C)
    total = None
    count = q_ref.shape[0] // C
    for n in reversed(range(count)):
        attn = attn_ref[cut(n), :]
        s, c = s_ref[cut(n), :], c_ref[cut(n), :]
        sg = s * gain
        normed_ref[cut(n), :] = (attn * sg).astype(BF16)
        grad = sg * g_ref[cut(n), :].astype(F32) - c * attn
        hi, lo = split(grad)
        hi_ref[cut(n), :] = hi
        lo_ref[cut(n), :] = lo
        qt = q_ref[cut(n), :].T
        part = nn(lanes(qt, qt), tall(grad * qd))
        grad_ref[n] = jnp.zeros((D, D), F32) if total is None else total
        total = part if total is None else total * step + part
    return total


def backward(q_ref, k_ref, v_ref, hi_ref, lo_ref, full_ref, grad_ref, tab, dq_ref, dk_ref, dv_ref):
    low, up, qd, kd = tab
    for n in range(q_ref.shape[0] // C):
        q, k, v = q_ref[cut(n), :], k_ref[cut(n), :], v_ref[cut(n), :]
        hi, lo = hi_ref[cut(n), :], lo_ref[cut(n), :]
        do = lanes(hi, lo)
        v2 = lanes(v, v)
        da = nt(do, v2) * low
        sh, sl = split(full_ref[n])
        ds = nt(do, rows(lanes(sh, sh), lanes(sl, sl)))
        dq = nn(wide(da), rows(k, k)) + qd * (ds[:, :D] + ds[:, D:])
        dq_ref[cut(n), :] = dq.astype(BF16)
        back = grad_ref[n]
        bh, bl = split(back)
        db = nt(v2, do) * up
        dk = nn(wide(db), rows(q, q)) + kd * nt(v2, lanes(bh, bl))
        dk_ref[cut(n), :] = dk.astype(BF16)
        pt = nt(k, q) * up
        dv2 = nn(wide(pt), rows(do, do))
        dv = dv2[:, :D] + dv2[:, D:] + kd * nn(lanes(k, k), rows(bh, bl))
        dv_ref[cut(n), :] = dv.astype(BF16)


def call(kernel, grid, ins, outs, scratch=()):
    return pl.pallas_call(
        kernel,
        grid=grid,
        in_specs=[spec for spec, _ in ins],
        out_specs=[spec for spec, _ in outs],
        out_shape=[shape for _, shape in outs],
        scratch_shapes=scratch,
        compiler_params=pltpu.CompilerParams(vmem_limit_bytes=48 * 1024 * 1024),
    )(*[arr for _, arr in ins])


SMEM = pl.BlockSpec(memory_space=pltpu.SMEM)


def local(q, k, v, g, pk, pv, which, sizes, decay, gain, features):
    rolls, length, width = q.shape
    heads = width // D
    count = length // C
    gain2 = gain.reshape(1, width)
    tok = pl.BlockSpec((1, length, D), lambda r, h: (r, 0, h))
    ptok = pl.BlockSpec((1, length, D), lambda h: (0, 0, h))
    gspec = pl.BlockSpec((1, D), lambda r, h: (0, h))
    stat = pl.BlockSpec((1, 1, count, D, D), lambda r, h: (r, h, 0, 0, 0))
    shape = jax.ShapeDtypeStruct
    states_shape = shape((rolls, heads, count, D, D), F32)

    def prompt_kernel(dec, kp, vp, out):
        e = dec[pl.program_id(0)]
        kd = tables(e)[3]
        out[0] = state_of_prompt(kp.at[0], vp.at[0], kd, e)

    (state,) = call(
        prompt_kernel, (heads,), [(SMEM, decay), (ptok, pk), (ptok, pv)],
        [(pl.BlockSpec((1, D, D), lambda h: (h, 0, 0)), shape((heads, D, D), F32))],
    )
    states = lax.all_gather(state, "roll")

    def local_kernel(dec, qr, kr, vr, out, st):
        e = dec[pl.program_id(1)]
        forward_local(qr.at[0], kr.at[0], vr.at[0], tables(e), e, out.at[0], st.at[0, 0])

    out_local, state_local = call(
        local_kernel, (rolls, heads), [(SMEM, decay), (tok, q), (tok, k), (tok, v)],
        [(tok, shape(q.shape, F32)), (stat, states_shape)],
    )

    def start_kernel(dec, wh, sz, qr, gr, gn, out, st, all_states, attn, full, msg, sq, cr):
        r, h = pl.program_id(0), pl.program_id(1)
        e = dec[h]
        start = all_states[wh[r], 0]
        forward_start(qr.at[0], gr.at[0], out.at[0], st.at[0, 0], start, gn[...].astype(F32), sz[r], tables(e), e,
                      attn.at[0], full.at[0, 0], sq, cr, h == 0)

        @pl.when(h == heads - 1)
        def _():
            msg[0, 0:1, :] = row_sums(sq[...])[0:1]
            msg[0, 1:2, :] = row_sums(cr[...])[0:1]

    attn, full, msg = call(
        start_kernel, (rolls, heads),
        [(SMEM, decay), (SMEM, which), (SMEM, sizes), (tok, q), (tok, g), (gspec, gain2), (tok, out_local), (stat, state_local),
         (pl.BlockSpec((states.shape[0], 1, D, D), lambda r, h: (0, h, 0, 0)), states)],
        [(tok, shape(q.shape, F32)), (stat, states_shape), (pl.BlockSpec((1, 2, length), lambda r, h: (r, 0, 0)), shape((rolls, 2, length), F32))],
        [pltpu.VMEM((length, D), F32), pltpu.VMEM((length, D), F32)],
    )
    sums = lax.psum(msg, "head")

    def back_kernel(dec, wh, sz, qr, gr, gn, at, sm, normed, hi, lo, gst, picked, sb, cb):
        r, h = pl.program_id(1), pl.program_id(0)
        e = dec[h]
        ss, cross = sm[0, 0:1, :], sm[0, 1:2, :]
        token = lax.broadcasted_iota(jnp.int32, (1, length), 1)
        scale = lax.rsqrt(ss / features + EPS)
        scale = jnp.where(token < sz[r], scale, 0.0)
        coef = scale * scale * scale * cross / features
        for n in range(count):
            sb[cut(n), :] = column(scale[:, n * C:(n + 1) * C])
            cb[cut(n), :] = column(coef[:, n * C:(n + 1) * C])
        total = start_back(qr.at[0], gr.at[0], at.at[0], sb, cb, gn[...].astype(F32), tables(e), e, normed.at[0], hi.at[0], lo.at[0], gst.at[0, 0])
        for p in range(states.shape[0]):
            old = jnp.where(r == 0, 0.0, picked[p, 0])
            picked[p, 0] = old + jnp.where(wh[r] == p, total, 0.0)

    tok2 = pl.BlockSpec((1, length, D), lambda h, r: (r, 0, h))
    stat2 = pl.BlockSpec((1, 1, count, D, D), lambda h, r: (r, h, 0, 0, 0))
    normed, hi, lo, back, picked = call(
        back_kernel, (heads, rolls),
        [(SMEM, decay), (SMEM, which), (SMEM, sizes), (tok2, q), (tok2, g), (pl.BlockSpec((1, D), lambda h, r: (0, h)), gain2), (tok2, attn),
         (pl.BlockSpec((1, 2, length), lambda h, r: (r, 0, 0)), sums)],
        [(tok2, shape(q.shape, BF16)), (tok2, shape(q.shape, BF16)), (tok2, shape(q.shape, BF16)), (stat2, states_shape),
         (pl.BlockSpec((states.shape[0], 1, D, D), lambda h, r: (0, h, 0, 0)), shape(states.shape, F32))],
        [pltpu.VMEM((length, D), F32), pltpu.VMEM((length, D), F32)],
    )
    owned = lax.psum_scatter(picked, "roll", scatter_dimension=0, tiled=True)

    def grads_kernel(dec, qr, kr, vr, hr, lr, fl, bk, dq, dk, dv):
        e = dec[pl.program_id(1)]
        backward(qr.at[0], kr.at[0], vr.at[0], hr.at[0], lr.at[0], fl.at[0, 0], bk.at[0, 0], tables(e), dq.at[0], dk.at[0], dv.at[0])

    dq, dk, dv = call(
        grads_kernel, (rolls, heads),
        [(SMEM, decay), (tok, q), (tok, k), (tok, v), (tok, hi), (tok, lo), (stat, full), (stat, back)],
        [(tok, shape(q.shape, BF16))] * 3,
    )

    def last_kernel(dec, kp, vp, gr, gk, gv):
        e = dec[pl.program_id(0)]
        prompt_grads(kp.at[0], vp.at[0], gr[0, 0], tables(e)[3], e, gk.at[0], gv.at[0])

    gkp, gvp = call(
        last_kernel, (heads,),
        [(SMEM, decay), (ptok, pk), (ptok, pv), (pl.BlockSpec((1, 1, D, D), lambda h: (0, h, 0, 0)), owned)],
        [(ptok, shape(pk.shape, BF16))] * 2,
    )
    return normed, dq, dk, dv, gkp, gvp


def solution(mesh):
    wide_spec = P("roll", None, "head")

    def run(q, k, v, g, pk, pv, which, sizes, decay, gain):
        body = functools.partial(local, features=gain.shape[0])
        return jax.shard_map(
            body,
            mesh=mesh,
            in_specs=(wide_spec,) * 6 + (P("roll"), P("roll"), P("head"), P("head")),
            out_specs=(wide_spec,) * 6,
            check_vma=False,
        )(q, k, v, g, pk, pv, which, sizes, decay, gain)

    return run
```

```python
import functools

import jax
import jax.numpy as jnp
from jax import lax
from jax.experimental import pallas as pl
from jax.experimental.pallas import tpu as pltpu
from jax.sharding import PartitionSpec as P

F32 = jnp.float32
BF16 = jnp.bfloat16
EPS = 1e-06
D = 128
C = 128


def nn(a, b):
    return lax.dot_general(a, b, (((1,), (0,)), ((), ())), preferred_element_type=F32)


def nt(a, b):
    return lax.dot_general(a, b, (((1,), (1,)), ((), ())), preferred_element_type=F32)


def lanes(a, b):
    return jnp.concatenate([a, b], axis=1)


def rows(a, b):
    return jnp.concatenate([a, b], axis=0)


def split(x):
    hi = x.astype(BF16)
    return hi, (x - hi.astype(F32)).astype(BF16)


def wide(x):
    return lanes(*split(x))


def tall(x):
    return rows(*split(x))


def rate_of(exponent, shape):
    return jnp.exp2(-jnp.full(shape, exponent, jnp.int32).astype(F32))


def tables(exponent):
    rate = rate_of(exponent, (C, C))
    i = lax.broadcasted_iota(jnp.int32, (C, C), 0).astype(F32)
    j = lax.broadcasted_iota(jnp.int32, (C, C), 1).astype(F32)
    gap = i - j
    decay = jnp.exp(-rate * jnp.abs(gap))
    low = jnp.where(gap >= 0.0, decay, 0.0)
    up = jnp.where(gap <= 0.0, decay, 0.0)
    qd = jnp.exp(-rate * (i + 1.0))
    kd = jnp.exp(-rate * (C - 1.0 - i))
    return low, up, qd, kd


def power(exponent, tokens):
    return jnp.exp(-rate_of(exponent, (1, D)) * float(tokens))


def cut(n):
    return pl.ds(n * C, C)


def state_of_prompt(kp, vp, kd, exponent):
    count = kp.shape[0] // C
    total = None
    for n in range(count):
        vd = vp[cut(n), :].astype(F32) * (kd * power(exponent, C * (count - 1 - n)))
        kt = kp[cut(n), :].T
        part = nn(lanes(kt, kt), tall(vd))
        total = part if total is None else total + part
    return total


def prompt_grads(kp, vp, grad, kd, exponent, gk_ref, gv_ref):
    count = kp.shape[0] // C
    flat, high = wide(grad), tall(grad)
    for n in range(count):
        decay = kd * power(exponent, C * (count - 1 - n))
        k, v = kp[cut(n), :], vp[cut(n), :]
        gk_ref[cut(n), :] = (nt(lanes(v, v), flat) * decay).astype(BF16)
        gv_ref[cut(n), :] = (nn(lanes(k, k), high) * decay).astype(BF16)


def forward_local(q_ref, k_ref, v_ref, tab, exponent, out_ref, state_ref):
    low, up, qd, kd = tab
    step = power(exponent, C)
    state = None
    for n in range(q_ref.shape[0] // C):
        q, k, v = q_ref[cut(n), :], k_ref[cut(n), :], v_ref[cut(n), :]
        out = nn(wide(nt(q, k) * low), rows(v, v))
        kt = k.T
        part = nn(lanes(kt, kt), tall(v.astype(F32) * kd))
        if n == 0:
            state_ref[n] = jnp.zeros((D, D), F32)
            state = part
        else:
            state_ref[n] = state
            out = out + qd * nn(lanes(q, q), tall(state))
            state = state * step + part
        out_ref[cut(n), :] = out


def forward_start(q_ref, g_ref, out_ref, state_ref, start, gain, size, tab, exponent, attn_ref, full_ref, sq_ref, cr_ref, first):
    low, up, qd, kd = tab
    high = tall(start)
    for n in range(q_ref.shape[0] // C):
        q = q_ref[cut(n), :]
        token = lax.broadcasted_iota(jnp.int32, (C, D), 0) + n * C
        lift = power(exponent, C * n)
        attn = out_ref[cut(n), :] + nn(lanes(q, q), high) * (qd * lift)
        attn = jnp.where(token < size, attn, 0.0)
        attn_ref[cut(n), :] = attn
        full_ref[n] = state_ref[n] + start * lift
        dyg = g_ref[cut(n), :].astype(F32) * gain
        square, cross = attn * attn, dyg * attn
        sq_ref[cut(n), :] = jnp.where(first, 0.0, sq_ref[cut(n), :]) + square
        cr_ref[cut(n), :] = jnp.where(first, 0.0, cr_ref[cut(n), :]) + cross


def row_sums(x):
    return nt(jnp.ones((8, 2 * D), BF16), wide(x))


def column(row):
    i = lax.broadcasted_iota(jnp.int32, (C, C), 0)
    j = lax.broadcasted_iota(jnp.int32, (C, C), 1)
    spread = jnp.where(i == j, row, 0.0)
    return nn(wide(spread), jnp.ones((2 * C, D), BF16))


def start_back(q_ref, g_ref, attn_ref, s_ref, c_ref, gain, tab, exponent, normed_ref, hi_ref, lo_ref, grad_ref):
    low, up, qd, kd = tab
    step = power(exponent, C)
    total = None
    count = q_ref.shape[0] // C
    for n in reversed(range(count)):
        attn = attn_ref[cut(n), :]
        s, c = s_ref[cut(n), :], c_ref[cut(n), :]
        sg = s * gain
        normed_ref[cut(n), :] = (attn * sg).astype(BF16)
        grad = sg * g_ref[cut(n), :].astype(F32) - c * attn
        hi, lo = split(grad)
        hi_ref[cut(n), :] = hi
        lo_ref[cut(n), :] = lo
        qt = q_ref[cut(n), :].T
        part = nn(lanes(qt, qt), tall(grad * qd))
        grad_ref[n] = jnp.zeros((D, D), F32) if total is None else total
        total = part if total is None else total * step + part
    return total


def backward(q_ref, k_ref, v_ref, hi_ref, lo_ref, full_ref, grad_ref, tab, dq_ref, dk_ref, dv_ref):
    low, up, qd, kd = tab
    for n in range(q_ref.shape[0] // C):
        q, k, v = q_ref[cut(n), :], k_ref[cut(n), :], v_ref[cut(n), :]
        hi, lo = hi_ref[cut(n), :], lo_ref[cut(n), :]
        do = lanes(hi, lo)
        v2 = lanes(v, v)
        da = nt(do, v2) * low
        sh, sl = split(full_ref[n])
        ds = nt(do, rows(lanes(sh, sh), lanes(sl, sl)))
        dq = nn(wide(da), rows(k, k)) + qd * (ds[:, :D] + ds[:, D:])
        dq_ref[cut(n), :] = dq.astype(BF16)
        back = grad_ref[n]
        bh, bl = split(back)
        db = nt(v2, do) * up
        dk = nn(wide(db), rows(q, q)) + kd * nt(v2, lanes(bh, bl))
        dk_ref[cut(n), :] = dk.astype(BF16)
        pt = nt(k, q) * up
        dv2 = nn(wide(pt), rows(do, do))
        dv = dv2[:, :D] + dv2[:, D:] + kd * nn(lanes(k, k), rows(bh, bl))
        dv_ref[cut(n), :] = dv.astype(BF16)


MESH = pl.DeviceIdType.MESH
SMEM = pl.BlockSpec(memory_space=pltpu.SMEM)
ANY = pl.BlockSpec(memory_space=pl.ANY)
ORDERS = ((0, 1, 2), (1, 2, 0), (2, 0, 1), (0, 1, 2))


def flip(place, dim, ring):
    if dim == 0:
        return (place + ring) % (2 * ring)
    if dim == 1:
        return place + 1 - 2 * (place % 2)
    return 2 * ring * (place // ring) + ring - 1 - place


def choose(number, blocks, owners):
    total = None
    for block, owner in zip(blocks, owners):
        part = jnp.where(number == owner, block, 0.0)
        total = part if total is None else total + part
    return total


def main_kernel(
    features, chips, ring,
    dec, wh, sz, gain_ref, q_hbm, k_hbm, v_hbm, g_hbm, pk_hbm, pv_hbm,
    normed_hbm, dq_hbm, dk_hbm, dv_hbm, owned_ref,
    q_ref, k_ref, v_ref, g_ref, pk_ref, pv_ref, out_ref, st_ref, back_ref, hi_ref, lo_ref,
    normed_ref, dq_ref, dk_ref, dv_ref, sq_ref, cr_ref, sb_ref, cb_ref, tab_ref,
    ag_ref, agsend_ref, agrecv_ref, start_ref, sg_ref, rs1_ref, acc_ref, rs2_ref, rs3_ref,
    tag_ref, tags_ref, msg_ref, core_ref, all_ref, sum_ref,
    in_sem, out_sem, tag_sem, ag_sem, rs_sem, ar_sem,
):
    rolls, length, width = q_ref.shape
    heads = width // D
    count = length // C
    me = lax.axis_index("roll")
    head_place = lax.axis_index("head")
    chip, core = head_place // 2, head_place % 2
    near = [flip(me, dim, ring) for dim in range(3)]
    sibling = chip * 2 + 1 - core
    others = [((chip + i) % chips) * 2 + core for i in range(1, chips)]

    loads = []
    for i, (src, dst) in enumerate(((pk_hbm.at[0], pk_ref), (pv_hbm.at[0], pv_ref), (k_hbm, k_ref), (v_hbm, v_ref), (q_hbm, q_ref), (g_hbm, g_ref))):
        copy = pltpu.make_async_copy(src, dst, in_sem.at[i])
        copy.start()
        loads.append(copy)

    barrier = pltpu.get_barrier_semaphore()
    for place in near:
        pl.semaphore_signal(barrier, inc=1, device_id={"roll": place, "head": head_place}, device_id_type=MESH)
    for place in [sibling] + others:
        pl.semaphore_signal(barrier, inc=1, device_id={"roll": me, "head": place}, device_id_type=MESH)

    def along_roll(src, dst, sems, slot, dim):
        return pltpu.make_async_remote_copy(
            src_ref=src, dst_ref=dst, send_sem=sems.at[0, slot], recv_sem=sems.at[1, slot],
            device_id={"roll": near[dim], "head": head_place}, device_id_type=MESH)

    def along_head(src, dst, sems, slot, place):
        return pltpu.make_async_remote_copy(
            src_ref=src, dst_ref=dst, send_sem=sems.at[0, slot], recv_sem=sems.at[1, slot],
            device_id={"roll": me, "head": place}, device_id_type=MESH)

    line = lax.broadcasted_iota(jnp.int32, (8, D), 0)
    tag_ref[...] = jnp.where(line == 0, wh[0], wh[1])

    def fill(h, _):
        low, up, qd, kd = tables(dec[h])
        tab_ref[h, 0] = low
        tab_ref[h, 1] = up
        tab_ref[h, 2] = qd
        tab_ref[h, 3] = kd
        return 0

    lax.fori_loop(0, heads, fill, 0)

    def tab_of(h):
        return tab_ref[h, 0], tab_ref[h, 1], tab_ref[h, 2], tab_ref[h, 3]

    def lane(h):
        return pl.ds(pl.multiple_of(h * D, D), D)

    loads[0].wait()
    loads[1].wait()
    pl.semaphore_wait(barrier, 3 + chips)

    tag_copies = [along_roll(tag_ref, tags_ref.at[dim], tag_sem, dim, dim) for dim in range(3)]
    for copy in tag_copies:
        copy.start()

    def gather(h, stage):
        dim = ORDERS[h][stage]
        src, dst = (
            (ag_ref.at[h, pl.ds(0, 1)], ag_ref.at[h, pl.ds(1, 1)]),
            (ag_ref.at[h, pl.ds(0, 2)], ag_ref.at[h, pl.ds(2, 2)]),
            (agsend_ref.at[h], agrecv_ref.at[h]),
        )[stage]
        return along_roll(src, dst, ag_sem, 3 * h + stage, dim)

    def owners_of(h):
        first, second, third = ORDERS[h]
        one = flip(me, first, ring)
        return [me, one, flip(me, second, ring), flip(one, second, ring)]

    gathers = [[gather(h, stage) for stage in range(3)] for h in range(heads)]
    for h in range(heads):
        def make_state(h):
            ag_ref[h, 0] = state_of_prompt(pk_ref.at[:, lane(h)], pv_ref.at[:, lane(h)], tab_ref[h, 3], dec[h])
        make_state(h)
        gathers[h][0].start()

    for copy in loads[2:5]:
        copy.wait()

    def local_unit(u, _):
        h, r = u // rolls, u % rolls
        view = (r, slice(None), lane(h))
        forward_local(q_ref.at[view], k_ref.at[view], v_ref.at[view], tab_of(h), dec[h], out_ref.at[view], st_ref.at[u])
        return 0

    units = heads * rolls
    lax.fori_loop(0, 2, local_unit, 0)
    for h in range(heads):
        gathers[h][0].wait()
        gathers[h][1].start()
    lax.fori_loop(2, 5, local_unit, 0)
    for copy in tag_copies:
        copy.wait()
    for h in range(heads):
        gathers[h][1].wait()
        tags = tags_ref[ORDERS[h][2]]
        for r in range(rolls):
            agsend_ref[h, r] = choose(tags[r:r + 1, :], [ag_ref[h, k] for k in range(4)], owners_of(h))
        gathers[h][2].start()
    lax.fori_loop(5, units, local_unit, 0)
    loads[5].wait()

    for h in range(heads):
        gathers[h][2].wait()
        for r in range(rolls):
            start_ref[h, r] = agrecv_ref[h, r] + choose(wh[r], [ag_ref[h, k] for k in range(4)], owners_of(h))

        def start_unit(r, _):
            view = (r, slice(None), pl.ds(h * D, D))
            gain = gain_ref[:, h * D:(h + 1) * D].astype(F32)
            forward_start(q_ref.at[view], g_ref.at[view], out_ref.at[view], st_ref.at[h * rolls + r], start_ref[h, r], gain, sz[r],
                          tab_of(h), dec[h], out_ref.at[view], st_ref.at[h * rolls + r], sq_ref.at[r], cr_ref.at[r], h == 0)
            return 0

        lax.fori_loop(0, rolls, start_unit, 0)

    def pack(total):
        packed = None
        for n in range(count):
            part = jnp.where(line == n, total[:, n * C:(n + 1) * C], 0.0)
            packed = part if packed is None else packed + part
        return packed

    for r in range(rolls):
        msg_ref[r, 0:8] = pack(row_sums(sq_ref[r]))
        msg_ref[r, 8:16] = pack(row_sums(cr_ref[r]))
    swap = along_head(msg_ref.at[1 - core], core_ref.at[0], ar_sem, 0, sibling)
    swap.start()
    swap.wait()
    all_ref[0] = msg_ref[core] + core_ref[0]
    pushes = [along_head(all_ref.at[0], all_ref.at[i], ar_sem, i, others[i - 1]) for i in range(1, chips)]
    for copy in pushes:
        copy.start()
    for copy in pushes:
        copy.wait()
    total = all_ref[0]
    for i in range(1, chips):
        total = total + all_ref[i]
    sum_ref[core] = total
    share = along_head(sum_ref.at[core], sum_ref.at[core], ar_sem, chips, sibling)
    share.start()
    share.wait()

    for r in range(rolls):
        ss, cross = sum_ref[r, 0:8], sum_ref[r, 8:16]
        token = line * C + lax.broadcasted_iota(jnp.int32, (8, D), 1)
        scale = jnp.where(token < sz[r], lax.rsqrt(ss / features + EPS), 0.0)
        coef = scale * scale * scale * cross / features
        for n in range(count):
            sb_ref[r, cut(n), :] = column(scale[n:n + 1, :])
            cb_ref[r, cut(n), :] = column(coef[n:n + 1, :])

    def scatter(h, stage):
        dim = ORDERS[h][2 - stage]
        src, dst = (
            (sg_ref.at[h], rs1_ref.at[h]),
            (acc_ref.at[h, pl.ds(2, 2)], rs2_ref.at[h]),
            (acc_ref.at[h, pl.ds(1, 1)], rs3_ref.at[h]),
        )[stage]
        return along_roll(src, dst, rs_sem, 3 * h + stage, dim)

    scatters = [[scatter(h, stage) for stage in range(3)] for h in range(heads)]
    for h in range(heads):
        def back_unit(r, _):
            view = (r, slice(None), pl.ds(h * D, D))
            gain = gain_ref[:, h * D:(h + 1) * D].astype(F32)
            sg_ref[h, r] = start_back(q_ref.at[view], g_ref.at[view], out_ref.at[view], sb_ref.at[r], cb_ref.at[r], gain, tab_of(h), dec[h],
                                      normed_ref.at[view], hi_ref.at[view], lo_ref.at[view], back_ref.at[h * rolls + r])
            return 0

        lax.fori_loop(0, rolls, back_unit, 0)
        scatters[h][0].start()

    stores = [pltpu.make_async_copy(normed_ref, normed_hbm, out_sem.at[0])]
    stores[0].start()

    def back_unit2(u, _):
        h, r = u // rolls, u % rolls
        view = (r, slice(None), lane(h))
        backward(q_ref.at[view], k_ref.at[view], v_ref.at[view], hi_ref.at[view], lo_ref.at[view], st_ref.at[u], back_ref.at[u], tab_of(h),
                 dq_ref.at[view], dk_ref.at[view], dv_ref.at[view])
        return 0

    lax.fori_loop(0, 2, back_unit2, 0)
    for h in range(heads):
        scatters[h][0].wait()
        tags = tags_ref[ORDERS[h][2]]
        for k, owner in enumerate(owners_of(h)):
            total = None
            for r in range(rolls):
                part = jnp.where(wh[r] == owner, sg_ref[h, r], 0.0) + jnp.where(tags[r:r + 1, :] == owner, rs1_ref[h, r], 0.0)
                total = part if total is None else total + part
            acc_ref[h, k] = total
        scatters[h][1].start()
    lax.fori_loop(2, 4, back_unit2, 0)
    for h in range(heads):
        scatters[h][1].wait()
        acc_ref[h, 0] += rs2_ref[h, 0]
        acc_ref[h, 1] += rs2_ref[h, 1]
        scatters[h][2].start()
    lax.fori_loop(4, units, back_unit2, 0)
    for i, (src, dst) in enumerate(((dq_ref, dq_hbm), (dk_ref, dk_hbm), (dv_ref, dv_hbm))):
        copy = pltpu.make_async_copy(src, dst, out_sem.at[1 + i])
        copy.start()
        stores.append(copy)
    for h in range(heads):
        scatters[h][2].wait()
        owned_ref[h] = acc_ref[h, 0] + rs3_ref[h, 0]
    for copy in stores:
        copy.wait()


def local(q, k, v, g, pk, pv, which, sizes, decay, gain, features, chips, ring):
    rolls, length, width = q.shape
    heads = width // D
    count = length // C
    units = heads * rolls
    shape = jax.ShapeDtypeStruct
    tokens = pltpu.VMEM(q.shape, BF16)
    block = lambda *lead: pltpu.VMEM((*lead, D, D), F32)
    dma = lambda *dims: pltpu.SemaphoreType.DMA(dims)
    normed, dq, dk, dv, owned = pl.pallas_call(
        functools.partial(main_kernel, features, chips, ring),
        in_specs=[SMEM, SMEM, SMEM, pl.BlockSpec(memory_space=pltpu.VMEM)] + [ANY] * 6,
        out_specs=[ANY] * 4 + [pl.BlockSpec(memory_space=pltpu.VMEM)],
        out_shape=[shape(q.shape, BF16)] * 4 + [shape((heads, D, D), F32)],
        scratch_shapes=[tokens] * 4 + [pltpu.VMEM((length, width), BF16)] * 2 + [pltpu.VMEM(q.shape, F32)]
        + [block(units, count)] * 2 + [tokens] * 6 + [pltpu.VMEM((rolls, length, D), F32)] * 4 + [block(heads, 4)]
        + [block(heads, 4), block(heads, 2), block(heads, 2), block(heads, 2)]
        + [block(heads, 2), block(heads, 2), block(heads, 4), block(heads, 2), block(heads, 1)]
        + [pltpu.VMEM((8, D), jnp.int32), pltpu.VMEM((3, 8, D), jnp.int32)]
        + [pltpu.VMEM((rolls, 16, D), F32), pltpu.VMEM((1, 16, D), F32), pltpu.VMEM((chips, 16, D), F32), pltpu.VMEM((rolls, 16, D), F32)]
        + [dma(6), dma(4), dma(2, 3), dma(2, 3 * heads), dma(2, 3 * heads), dma(2, chips + 1)],
        compiler_params=pltpu.CompilerParams(vmem_limit_bytes=60 * 1024 * 1024, collective_id=0, has_side_effects=True),
    )(decay, which, sizes, gain.reshape(1, width), q, k, v, g, pk, pv)

    def last_kernel(dec, kp, vp, gr, gk, gv):
        e = dec[pl.program_id(0)]
        prompt_grads(kp.at[0], vp.at[0], gr[0], tables(e)[3], e, gk.at[0], gv.at[0])

    ptok = pl.BlockSpec((1, length, D), lambda h: (0, 0, h))
    gkp, gvp = pl.pallas_call(
        last_kernel,
        grid=(heads,),
        in_specs=[SMEM, ptok, ptok, pl.BlockSpec((1, D, D), lambda h: (h, 0, 0))],
        out_specs=[ptok] * 2,
        out_shape=[shape(pk.shape, BF16)] * 2,
        compiler_params=pltpu.CompilerParams(vmem_limit_bytes=32 * 1024 * 1024),
    )(decay, pk, pv, owned)
    return normed, dq, dk, dv, gkp, gvp


def solution(mesh):
    wide_spec = P("roll", None, "head")
    chips = mesh.shape["head"] // 2
    ring = mesh.shape["roll"] // 2

    def run(q, k, v, g, pk, pv, which, sizes, decay, gain):
        body = functools.partial(local, features=gain.shape[0], chips=chips, ring=ring)
        return jax.shard_map(
            body,
            mesh=mesh,
            in_specs=(wide_spec,) * 6 + (P("roll"), P("roll"), P("head"), P("head")),
            out_specs=(wide_spec,) * 6,
            check_vma=False,
        )(q, k, v, g, pk, pv, which, sizes, decay, gain)

    return run
```

```python
import functools

import jax
import jax.numpy as jnp
from jax import lax
from jax.experimental import pallas as pl
from jax.experimental.pallas import tpu as pltpu
from jax.sharding import PartitionSpec as P

F32 = jnp.float32
BF16 = jnp.bfloat16
EPS = 1e-06
D = 128
C = 128


def nn(a, b):
    return lax.dot_general(a, b, (((1,), (0,)), ((), ())), preferred_element_type=F32)


def nt(a, b):
    return lax.dot_general(a, b, (((1,), (1,)), ((), ())), preferred_element_type=F32)


def lanes(a, b):
    return jnp.concatenate([a, b], axis=1)


def rows(a, b):
    return jnp.concatenate([a, b], axis=0)


def split(x):
    hi = x.astype(BF16)
    return hi, (x - hi.astype(F32)).astype(BF16)


def wide(x):
    return lanes(*split(x))


def tall(x):
    return rows(*split(x))


def rate_of(exponent, shape):
    return jnp.exp2(-jnp.full(shape, exponent, jnp.int32).astype(F32))


def tables(exponent):
    rate = rate_of(exponent, (C, C))
    i = lax.broadcasted_iota(jnp.int32, (C, C), 0).astype(F32)
    j = lax.broadcasted_iota(jnp.int32, (C, C), 1).astype(F32)
    gap = i - j
    decay = jnp.exp(-rate * jnp.abs(gap))
    low = jnp.where(gap >= 0.0, decay, 0.0)
    up = jnp.where(gap <= 0.0, decay, 0.0)
    qd = jnp.exp(-rate * (i + 1.0))
    kd = jnp.exp(-rate * (C - 1.0 - i))
    return low, up, qd, kd


def power(exponent, tokens):
    return jnp.exp(-rate_of(exponent, (1, D)) * float(tokens))


def cut(n):
    return pl.ds(n * C, C)


def state_of_prompt(kp, vp, kd, exponent):
    count = kp.shape[0] // C
    total = None
    for n in range(count):
        vd = vp[cut(n), :].astype(F32) * (kd * power(exponent, C * (count - 1 - n)))
        kt = kp[cut(n), :].T
        part = nn(lanes(kt, kt), tall(vd))
        total = part if total is None else total + part
    return total


def prompt_grads(kp, vp, grad, kd, exponent, gk_ref, gv_ref):
    count = kp.shape[0] // C
    flat, high = wide(grad), tall(grad)
    for n in range(count):
        decay = kd * power(exponent, C * (count - 1 - n))
        k, v = kp[cut(n), :], vp[cut(n), :]
        gk_ref[cut(n), :] = (nt(lanes(v, v), flat) * decay).astype(BF16)
        gv_ref[cut(n), :] = (nn(lanes(k, k), high) * decay).astype(BF16)


def forward_local(q_ref, k_ref, v_ref, tab, exponent, out_ref, state_ref):
    low, up, qd, kd = tab
    step = power(exponent, C)
    zero = jnp.zeros((D, C), BF16)
    count = q_ref.shape[0] // C
    state_ref[0] = jnp.zeros((D, D), F32)
    state = None
    for n in range(count - 1):
        kt = k_ref[cut(n), :].T
        part = nn(lanes(kt, kt), tall(v_ref[cut(n), :].astype(F32) * kd))
        state = part if n == 0 else state * step + part
        state_ref[n + 1] = state
    for n in range(count):
        q, k, v = q_ref[cut(n), :], k_ref[cut(n), :], v_ref[cut(n), :]
        kt = k.T
        if n == 0:
            out = nn(wide(nn(q, kt) * low), rows(v, v))
        else:
            both = nn(lanes(q, q), lanes(rows(kt, zero), tall(state_ref[n])))
            out = nn(wide(both[:, :C] * low), rows(v, v)) + qd * both[:, C:]
        out_ref[cut(n), :] = out


def forward_start(q_ref, g_ref, attn_ref, start, gain, size, tab, exponent, sq_ref, cr_ref, first):
    low, up, qd, kd = tab
    high = tall(start)
    for n in range(q_ref.shape[0] // C):
        q = q_ref[cut(n), :]
        token = lax.broadcasted_iota(jnp.int32, (C, D), 0) + n * C
        attn = attn_ref[cut(n), :] + nn(lanes(q, q), high) * (qd * power(exponent, C * n))
        attn = jnp.where(token < size, attn, 0.0)
        attn_ref[cut(n), :] = attn
        dyg = g_ref[cut(n), :].astype(F32) * gain
        square, cross = attn * attn, dyg * attn
        sq_ref[cut(n), :] = jnp.where(first, 0.0, sq_ref[cut(n), :]) + square
        cr_ref[cut(n), :] = jnp.where(first, 0.0, cr_ref[cut(n), :]) + cross


def ready(q_ref, state_ref, qs_ref, start, tab, exponent):
    low, up, qd, kd = tab
    for n in range(q_ref.shape[0] // C):
        state_ref[n] = state_ref[n] + start * power(exponent, C * n)
        hi, lo = split(q_ref[cut(n), :].astype(F32) * qd)
        qs_ref[n] = lanes(hi.T, lo.T)


def row_sums(x):
    return nt(jnp.ones((8, 2 * D), BF16), wide(x))


def column(row):
    i = lax.broadcasted_iota(jnp.int32, (C, C), 0)
    j = lax.broadcasted_iota(jnp.int32, (C, C), 1)
    spread = jnp.where(i == j, row, 0.0)
    return nn(wide(spread), jnp.ones((2 * C, D), BF16))


def start_back(qs_ref, g_ref, attn_ref, s_ref, c_ref, gain, exponent, hi_ref, lo_ref, grad_ref):
    step = power(exponent, C)
    total = None
    count = qs_ref.shape[0]
    for n in reversed(range(count)):
        attn = attn_ref[cut(n), :]
        s, c = s_ref[cut(n), :], c_ref[cut(n), :]
        hi, lo = split(s * gain * g_ref[cut(n), :].astype(F32) - c * attn)
        hi_ref[cut(n), :] = hi
        lo_ref[cut(n), :] = lo
        do = lanes(hi, lo)
        both = nn(qs_ref[n], rows(do, do))
        part = both[:, :D] + both[:, D:]
        grad_ref[n] = jnp.zeros((D, D), F32) if total is None else total
        total = part if total is None else total * step + part
    return total


def backward(q_ref, k_ref, v_ref, hi_ref, lo_ref, full_ref, grad_ref, tab, dq_ref, dk_ref, dv_ref):
    low, up, qd, kd = tab
    zero = jnp.zeros((D, C), BF16)
    for n in range(q_ref.shape[0] // C):
        q, k, v = q_ref[cut(n), :], k_ref[cut(n), :], v_ref[cut(n), :]
        hi, lo = hi_ref[cut(n), :], lo_ref[cut(n), :]
        do = lanes(hi, lo)
        vt = v.T
        sh, sl = split(full_ref[n])
        flat = lanes(vt, sh.T)
        both = nn(do, rows(flat, flat))
        ds = both[:, D:] + nn(hi, sl.T)
        dq = nn(wide(both[:, :D] * low), rows(k, k)) + qd * ds
        dq_ref[cut(n), :] = dq.astype(BF16)
        bh, bl = split(grad_ref[n])
        vb = nn(lanes(v, v), rows(lanes(hi.T, bh.T), lanes(lo.T, bl.T)))
        dk = nn(wide(vb[:, :C] * up), rows(q, q)) + kd * vb[:, C:]
        dk_ref[cut(n), :] = dk.astype(BF16)
        kb = nn(lanes(k, k), lanes(rows(q.T, zero), rows(bh, bl)))
        dv2 = nn(wide(kb[:, :C] * up), rows(do, do))
        dv = dv2[:, :D] + dv2[:, D:] + kd * kb[:, C:]
        dv_ref[cut(n), :] = dv.astype(BF16)


MESH = pl.DeviceIdType.MESH
SMEM = pl.BlockSpec(memory_space=pltpu.SMEM)
ANY = pl.BlockSpec(memory_space=pl.ANY)
TURNS = ((0, 1, 2), (1, 2, 0), (2, 0, 1))
PARTS = tuple((h, TURNS[h], 0, D) for h in range(3)) + ((3, TURNS[0], 0, 48), (3, TURNS[1], 48, 40), (3, TURNS[2], 88, 40))

def flip(place, dim, ring):
    if dim == 0:
        return (place + ring) % (2 * ring)
    if dim == 1:
        return place + 1 - 2 * (place % 2)
    return 2 * ring * (place // ring) + ring - 1 - place


def choose(number, blocks, owners):
    total = None
    for block, owner in zip(blocks, owners):
        part = jnp.where(number == owner, block, 0.0)
        total = part if total is None else total + part
    return total


def main_kernel(
    features, chips, ring,
    dec, wh, sz, gain_ref, q_hbm, k_hbm, v_hbm, g_hbm, pk_hbm, pv_hbm,
    normed_ref, dq_ref, dk_ref, dv_ref, owned_ref, pk_ref, pv_ref,
    q_ref, k_ref, v_ref, g_ref, out_ref, st_ref, back_ref, hi_ref, lo_ref, sq_ref, cr_ref, sb_ref, cb_ref, tab_ref,
    ag_ref, agsend_ref, agrecv_ref, start_ref, sg_ref, rs1_ref, acc_ref, rs2_ref, rs3_ref,
    qs_ref, gains_ref, tag_ref, tags_ref, msg_ref, all_ref,
    in_sem, tag_sem, ag_sem, rs_sem, ar_sem,
):
    rolls, length, width = q_ref.shape
    heads = width // D
    count = length // C
    me = lax.axis_index("roll")
    head_place = lax.axis_index("head")
    chip, core = head_place // 2, head_place % 2
    near = [flip(me, dim, ring) for dim in range(3)]
    others = [((chip + i) % chips) * 2 + side for i in range(chips) for side in (core, 1 - core)][1:]

    loads = []
    for i, (src, dst) in enumerate(((pk_hbm.at[0], pk_ref), (pv_hbm.at[0], pv_ref), (k_hbm, k_ref), (v_hbm, v_ref), (q_hbm, q_ref), (g_hbm, g_ref))):
        copy = pltpu.make_async_copy(src, dst, in_sem.at[i])
        copy.start()
        loads.append(copy)

    barrier = pltpu.get_barrier_semaphore()
    for place in near:
        pl.semaphore_signal(barrier, inc=1, device_id={"roll": place, "head": head_place}, device_id_type=MESH)
    for place in others:
        pl.semaphore_signal(barrier, inc=1, device_id={"roll": me, "head": place}, device_id_type=MESH)

    def along_roll(src, dst, sems, slot, dim):
        return pltpu.make_async_remote_copy(
            src_ref=src, dst_ref=dst, send_sem=sems.at[0, slot], recv_sem=sems.at[1, slot],
            device_id={"roll": near[dim], "head": head_place}, device_id_type=MESH)

    def along_head(src, dst, sems, slot, place):
        return pltpu.make_async_remote_copy(
            src_ref=src, dst_ref=dst, send_sem=sems.at[0, slot], recv_sem=sems.at[1, slot],
            device_id={"roll": me, "head": place}, device_id_type=MESH)

    line = lax.broadcasted_iota(jnp.int32, (8, D), 0)
    tag_ref[...] = jnp.where(line == 0, wh[0], wh[1])

    for h in range(heads):
        gains_ref[h] = gain_ref[pl.ds(h * D, D)].astype(F32).reshape(1, D)

    def fill(h, _):
        low, up, qd, kd = tables(dec[h])
        tab_ref[h, 0] = low
        tab_ref[h, 1] = up
        tab_ref[h, 2] = qd
        tab_ref[h, 3] = kd
        return 0

    lax.fori_loop(0, heads, fill, 0)

    def tab_of(h):
        return tab_ref[h, 0], tab_ref[h, 1], tab_ref[h, 2], tab_ref[h, 3]

    def lane(h):
        return pl.ds(pl.multiple_of(h * D, D), D)

    loads[0].wait()
    loads[1].wait()
    for h in range(heads):
        ag_ref[h, 0] = state_of_prompt(pk_ref.at[:, lane(h)], pv_ref.at[:, lane(h)], tab_ref[h, 3], dec[h])
    pl.semaphore_wait(barrier, 3 + len(others))

    tag_copies = [along_roll(tag_ref, tags_ref.at[dim], tag_sem, dim, dim) for dim in range(3)]
    for copy in tag_copies:
        copy.start()

    def owners_of(order):
        first, second, third = order
        one = flip(me, first, ring)
        return [me, one, flip(me, second, ring), flip(one, second, ring)]

    def gather(i, stage, r=0):
        h, order, low, size = PARTS[i]
        cells = pl.ds(low, size)
        src, dst, dim = (
            (ag_ref.at[h, 0, cells], ag_ref.at[h, 1, cells], order[0]),
            (ag_ref.at[h, 0, cells], ag_ref.at[h, 2, cells], order[1]),
            (ag_ref.at[h, 1, cells], ag_ref.at[h, 3, cells], order[1]),
            (agsend_ref.at[h, r, cells], agrecv_ref.at[h, r, cells], order[2]),
        )[stage]
        return along_roll(src, dst, ag_sem, 5 * i + stage + r, dim)

    for stage in range(2):
        for i in range(len(PARTS)):
            gather(i, stage).start()

    for copy in loads[2:5]:
        copy.wait()

    def local_unit(u, _):
        h, r = u // rolls, u % rolls
        view = (r, slice(None), lane(h))
        forward_local(q_ref.at[view], k_ref.at[view], v_ref.at[view], tab_of(h), dec[h], out_ref.at[view], st_ref.at[u])
        return 0

    units = heads * rolls
    def relay(begin, end):
        for i in range(begin, end):
            gather(i, 0).wait()
            gather(i, 2).start()

    lax.fori_loop(0, 3, local_unit, 0)
    relay(0, 3)
    lax.fori_loop(3, 5, local_unit, 0)
    relay(3, len(PARTS))
    lax.fori_loop(5, units, local_unit, 0)
    for copy in tag_copies:
        copy.wait()

    def send_start(i, r):
        h, order, low, size = PARTS[i]
        cells = pl.ds(low, size)
        tags = tags_ref[order[2]]
        agsend_ref[h, r, cells] = choose(tags[r:r + 1, :], [ag_ref[h, k, cells] for k in range(4)], owners_of(order))
        gather(i, 3, r).start()

    def take_start(i, r):
        h, order, low, size = PARTS[i]
        cells = pl.ds(low, size)
        gather(i, 3, r).wait()
        start_ref[h, r, cells] = agrecv_ref[h, r, cells] + choose(wh[r], [ag_ref[h, k, cells] for k in range(4)], owners_of(order))

    for begin, end in ((0, 3), (3, len(PARTS))):
        for i in range(begin, end):
            gather(i, 1).wait()
            gather(i, 2).wait()
            send_start(i, 0)
        for i in range(begin, end):
            send_start(i, 1)
    loads[5].wait()

    def start_units(r, begin, end):
        def unit(h, _):
            view = (r, slice(None), lane(h))
            forward_start(q_ref.at[view], g_ref.at[view], out_ref.at[view], start_ref[h, r], gains_ref[h], sz[r],
                          tab_of(h), dec[h], sq_ref.at[r], cr_ref.at[r], h == 0)
            return 0

        lax.fori_loop(begin, end, unit, 0)

    def pack(total):
        packed = None
        for n in range(count):
            part = jnp.where(line == n, total[:, n * C:(n + 1) * C], 0.0)
            packed = part if packed is None else packed + part
        return packed

    def push(r, i):
        return along_head(msg_ref.at[r], all_ref.at[r, i], ar_sem, len(others) * r + i, others[i])

    def open_sum(r):
        msg_ref[r, 0:8] = pack(row_sums(sq_ref[r]))
        msg_ref[r, 8:16] = pack(row_sums(cr_ref[r]))
        for i in range(len(others)):
            push(r, i).start()

    def close_sum(r):
        for i in range(len(others)):
            push(r, i).wait()
        total = msg_ref[r]
        for i in range(len(others)):
            total = total + all_ref[r, i]
        ss, cross = total[0:8], total[8:16]
        token = line * C + lax.broadcasted_iota(jnp.int32, (8, D), 1)
        scale = jnp.where(token < sz[r], lax.rsqrt(ss / features + EPS), 0.0)
        coef = scale * scale * scale * cross / features
        for n in range(count):
            sb_ref[r, cut(n), :] = column(scale[n:n + 1, :])
            cb_ref[r, cut(n), :] = column(coef[n:n + 1, :])

    def back_units(r, begin, end):
        def unit(h, _):
            view = (r, slice(None), lane(h))
            sg_ref[h, r] = start_back(qs_ref.at[h * rolls + r], g_ref.at[view], out_ref.at[view], sb_ref.at[r], cb_ref.at[r], gains_ref[h], dec[h],
                                      hi_ref.at[view], lo_ref.at[view], back_ref.at[h * rolls + r])
            return 0

        lax.fori_loop(begin, end, unit, 0)

    def scatter(i, stage):
        h, order, low, size = PARTS[i]
        cells = pl.ds(low, size)
        src, dst = (
            (sg_ref.at[h, :, cells], rs1_ref.at[h, :, cells]),
            (acc_ref.at[h, pl.ds(2, 2), cells], rs2_ref.at[h, :, cells]),
            (acc_ref.at[h, pl.ds(1, 1), cells], rs3_ref.at[h, :, cells]),
        )[stage]
        return along_roll(src, dst, rs_sem, 3 * i + stage, order[2 - stage])

    for r in range(rolls):
        for i in range(3):
            take_start(i, r)
        start_units(r, 0, 3)
        for i in range(3, len(PARTS)):
            take_start(i, r)
        start_units(r, 3, heads)
        open_sum(r)

    def ready_unit(u, _):
        h, r = u // rolls, u % rolls
        ready(q_ref.at[r, slice(None), lane(h)], st_ref.at[u], qs_ref.at[u], start_ref[h, r], tab_of(h), dec[h])
        return 0

    lax.fori_loop(0, units, ready_unit, 0)
    for r in range(rolls - 1):
        close_sum(r)
        back_units(r, 0, heads)
    close_sum(rolls - 1)
    for h in range(heads):
        back_units(rolls - 1, h, h + 1)
        for i, part in enumerate(PARTS):
            if part[0] == h:
                scatter(i, 0).start()

    def grad_unit(u, _):
        h, r = u // rolls, u % rolls
        view = (r, slice(None), lane(h))
        backward(q_ref.at[view], k_ref.at[view], v_ref.at[view], hi_ref.at[view], lo_ref.at[view], st_ref.at[u], back_ref.at[u], tab_of(h),
                 dq_ref.at[view], dk_ref.at[view], dv_ref.at[view])
        for n in range(count):
            cells = (r, cut(n), lane(h))
            normed_ref[cells] = (out_ref[cells] * sb_ref[r, cut(n), :] * gains_ref[h]).astype(BF16)
        return 0

    lax.fori_loop(0, 2, grad_unit, 0)
    for i, (h, order, low, size) in enumerate(PARTS):
        cells = pl.ds(low, size)
        tags = tags_ref[order[2]]
        scatter(i, 0).wait()
        for k, owner in enumerate(owners_of(order)):
            total = None
            for r in range(rolls):
                part = jnp.where(wh[r] == owner, sg_ref[h, r, cells], 0.0) + jnp.where(tags[r:r + 1, :] == owner, rs1_ref[h, r, cells], 0.0)
                total = part if total is None else total + part
            acc_ref[h, k, cells] = total
        scatter(i, 1).start()
    lax.fori_loop(2, 6, grad_unit, 0)
    for i, (h, order, low, size) in enumerate(PARTS):
        cells = pl.ds(low, size)
        scatter(i, 1).wait()
        acc_ref[h, 0, cells] += rs2_ref[h, 0, cells]
        acc_ref[h, 1, cells] += rs2_ref[h, 1, cells]
        scatter(i, 2).start()
    lax.fori_loop(6, units, grad_unit, 0)
    for i, (h, order, low, size) in enumerate(PARTS):
        cells = pl.ds(low, size)
        scatter(i, 2).wait()
        owned_ref[h, cells] = acc_ref[h, 0, cells] + rs3_ref[h, 0, cells]


def last_kernel(dec, normed, dq, dk, dv, grad, pk, pv, normed_hbm, dq_hbm, dk_hbm, dv_hbm, gk_hbm, gv_hbm, gk_ref, gv_ref, sem):
    copies = [pltpu.make_async_copy(src, dst, sem.at[i]) for i, (src, dst) in enumerate(
        ((normed, normed_hbm), (dq, dq_hbm), (dk, dk_hbm), (dv, dv_hbm), (gk_ref, gk_hbm.at[0]), (gv_ref, gv_hbm.at[0])))]
    for copy in copies[:4]:
        copy.start()

    def unit(h, _):
        view = (slice(None), pl.ds(pl.multiple_of(h * D, D), D))
        prompt_grads(pk.at[view], pv.at[view], grad[h], tables(dec[h])[3], dec[h], gk_ref.at[view], gv_ref.at[view])
        return 0

    lax.fori_loop(0, grad.shape[0], unit, 0)
    for copy in copies[4:]:
        copy.start()
    for copy in copies:
        copy.wait()


def local(q, k, v, g, pk, pv, which, sizes, decay, gain, features, chips, ring):
    rolls, length, width = q.shape
    heads = width // D
    count = length // C
    units = heads * rolls
    shape = jax.ShapeDtypeStruct
    vmem = pl.BlockSpec(memory_space=pltpu.VMEM)
    tokens = pltpu.VMEM(q.shape, BF16)
    prompt = pltpu.VMEM((length, width), BF16)
    block = lambda *lead: pltpu.VMEM((*lead, D, D), F32)
    dma = lambda *dims: pltpu.SemaphoreType.DMA(dims)
    parts = len(PARTS)
    made = pl.pallas_call(
        functools.partial(main_kernel, features, chips, ring),
        in_specs=[SMEM, SMEM, SMEM, vmem] + [ANY] * 6,
        out_specs=[vmem] * 7,
        out_shape=[tokens] * 4 + [block(heads)] + [prompt] * 2,
        scratch_shapes=[tokens] * 4 + [pltpu.VMEM(q.shape, F32)]
        + [block(units, count)] * 2 + [tokens] * 2 + [pltpu.VMEM((rolls, length, D), F32)] * 4 + [block(heads, 4)]
        + [block(heads, 4), block(heads, 2), block(heads, 2), block(heads, 2)]
        + [block(heads, 2), block(heads, 2), block(heads, 4), block(heads, 2), block(heads, 1)]
        + [pltpu.VMEM((units, count, D, 2 * C), BF16), pltpu.VMEM((heads, 1, D), F32), pltpu.VMEM((8, D), jnp.int32), pltpu.VMEM((3, 8, D), jnp.int32)]
        + [pltpu.VMEM((rolls, 16, D), F32), pltpu.VMEM((rolls, 2 * chips - 1, 16, D), F32)]
        + [dma(6), dma(2, 3), dma(2, 5 * parts), dma(2, 3 * parts), dma(2, rolls * (2 * chips - 1))],
        compiler_params=pltpu.CompilerParams(vmem_limit_bytes=44 * 1024 * 1024, collective_id=0, has_side_effects=True),
    )(decay, which, sizes, gain, q, k, v, g, pk, pv)

    return pl.pallas_call(
        last_kernel,
        in_specs=[SMEM] + [vmem] * 7,
        out_specs=[ANY] * 6,
        out_shape=[shape(q.shape, BF16)] * 4 + [shape(pk.shape, BF16)] * 2,
        scratch_shapes=[prompt] * 2 + [dma(6)],
        compiler_params=pltpu.CompilerParams(vmem_limit_bytes=8 * 1024 * 1024),
    )(decay, *made)


def solution(mesh):
    wide_spec = P("roll", None, "head")
    chips = mesh.shape["head"] // 2
    ring = mesh.shape["roll"] // 2

    def run(q, k, v, g, pk, pv, which, sizes, decay, gain):
        body = functools.partial(local, features=gain.shape[0], chips=chips, ring=ring)
        return jax.shard_map(
            body,
            mesh=mesh,
            in_specs=(wide_spec,) * 6 + (P("roll"), P("roll"), P("head"), P("head")),
            out_specs=(wide_spec,) * 6,
            check_vma=False,
        )(q, k, v, g, pk, pv, which, sizes, decay, gain)

    return run
```

```python
import functools

import jax
import jax.numpy as jnp
from jax import lax
from jax.experimental import pallas as pl
from jax.experimental.pallas import tpu as pltpu
from jax.sharding import PartitionSpec as P

F32 = jnp.float32
BF16 = jnp.bfloat16
EPS = 1e-06
D = 128
C = 128


def nn(a, b):
    return lax.dot_general(a, b, (((1,), (0,)), ((), ())), preferred_element_type=F32)


def nt(a, b):
    return lax.dot_general(a, b, (((1,), (1,)), ((), ())), preferred_element_type=F32)


def lanes(a, b):
    return jnp.concatenate([a, b], axis=1)


def rows(a, b):
    return jnp.concatenate([a, b], axis=0)


def split(x):
    hi = x.astype(BF16)
    return hi, (x - hi.astype(F32)).astype(BF16)


def wide(x):
    return lanes(*split(x))


def tall(x):
    return rows(*split(x))


def rate_of(exponent, shape):
    return jnp.exp2(-jnp.full(shape, exponent, jnp.int32).astype(F32))


def tables(exponent):
    rate = rate_of(exponent, (C, C))
    i = lax.broadcasted_iota(jnp.int32, (C, C), 0).astype(F32)
    j = lax.broadcasted_iota(jnp.int32, (C, C), 1).astype(F32)
    gap = i - j
    decay = jnp.exp(-rate * jnp.abs(gap))
    low = jnp.where(gap >= 0.0, decay, 0.0)
    up = jnp.where(gap <= 0.0, decay, 0.0)
    qd = jnp.exp(-rate * (i + 1.0))
    kd = jnp.exp(-rate * (C - 1.0 - i))
    return low, up, qd, kd


def powers(exponent, count):
    return jnp.exp(-rate_of(exponent, (count, D)) * (lax.broadcasted_iota(jnp.int32, (count, D), 0) * C).astype(F32))


def cut(n):
    return pl.ds(n * C, C)


def state_of_prompt(kp, vp, kd, pw):
    count = kp.shape[0] // C
    total = None
    for n in range(count):
        vd = vp[cut(n), :].astype(F32) * (kd * pw[count - 1 - n:count - n])
        kt = kp[cut(n), :].T
        part = nn(lanes(kt, kt), tall(vd))
        total = part if total is None else total + part
    return total


def prompt_grads(kp, vp, grad, kd, pw, gk_ref, gv_ref):
    count = kp.shape[0] // C
    flat, high = wide(grad), tall(grad)
    for n in range(count):
        decay = kd * pw[count - 1 - n:count - n]
        k, v = kp[cut(n), :], vp[cut(n), :]
        gk_ref[cut(n), :] = (nt(lanes(v, v), flat) * decay).astype(BF16)
        gv_ref[cut(n), :] = (nn(lanes(k, k), high) * decay).astype(BF16)


def forward_local(q_ref, k_ref, v_ref, tab, pw, out_ref, state_ref):
    low, up, qd, kd = tab
    step = pw[1:2]
    zero = jnp.zeros((D, C), BF16)
    count = q_ref.shape[0] // C
    state_ref[0] = jnp.zeros((D, D), F32)
    state = None
    for n in range(count - 1):
        kt = k_ref[cut(n), :].T
        part = nn(lanes(kt, kt), tall(v_ref[cut(n), :].astype(F32) * kd))
        state = part if n == 0 else state * step + part
        state_ref[n + 1] = state
    for n in range(count):
        q, k, v = q_ref[cut(n), :], k_ref[cut(n), :], v_ref[cut(n), :]
        kt = k.T
        if n == 0:
            out = nn(wide(nn(q, kt) * low), rows(v, v))
        else:
            both = nn(lanes(q, q), lanes(rows(kt, zero), tall(state_ref[n])))
            out = nn(wide(both[:, :C] * low), rows(v, v)) + qd * both[:, C:]
        out_ref[cut(n), :] = out


def forward_start(q_ref, g_ref, attn_ref, start, gain, size, tab, pw, sq_ref, cr_ref, first):
    low, up, qd, kd = tab
    high = tall(start)
    for n in range(q_ref.shape[0] // C):
        q = q_ref[cut(n), :]
        token = lax.broadcasted_iota(jnp.int32, (C, D), 0) + n * C
        attn = attn_ref[cut(n), :] + nn(lanes(q, q), high) * (qd * pw[n:n + 1])
        attn = jnp.where(token < size, attn, 0.0)
        attn_ref[cut(n), :] = attn
        dyg = g_ref[cut(n), :].astype(F32) * gain
        square, cross = attn * attn, dyg * attn
        sq_ref[cut(n), :] = jnp.where(first, 0.0, sq_ref[cut(n), :]) + square
        cr_ref[cut(n), :] = jnp.where(first, 0.0, cr_ref[cut(n), :]) + cross


def ready(q_ref, state_ref, qs_ref, start, tab, pw):
    low, up, qd, kd = tab
    for n in range(q_ref.shape[0] // C):
        state_ref[n] = state_ref[n] + start * pw[n:n + 1]
        hi, lo = split(q_ref[cut(n), :].astype(F32) * qd)
        qs_ref[n] = lanes(hi.T, lo.T)


def row_sums(x):
    return nt(jnp.ones((8, 2 * D), BF16), wide(x))


def column(row):
    i = lax.broadcasted_iota(jnp.int32, (C, C), 0)
    j = lax.broadcasted_iota(jnp.int32, (C, C), 1)
    spread = jnp.where(i == j, row, 0.0)
    return nn(wide(spread), jnp.ones((2 * C, D), BF16))


def start_back(qs_ref, g_ref, attn_ref, s_ref, c_ref, gain, pw, hi_ref, lo_ref, grad_ref):
    step = pw[1:2]
    total = None
    count = qs_ref.shape[0]
    for n in reversed(range(count)):
        attn = attn_ref[cut(n), :]
        s, c = s_ref[cut(n), :], c_ref[cut(n), :]
        hi, lo = split(s * gain * g_ref[cut(n), :].astype(F32) - c * attn)
        hi_ref[cut(n), :] = hi
        lo_ref[cut(n), :] = lo
        do = lanes(hi, lo)
        both = nn(qs_ref[n], rows(do, do))
        part = both[:, :D] + both[:, D:]
        grad_ref[n] = jnp.zeros((D, D), F32) if total is None else total
        total = part if total is None else total * step + part
    return total


def backward(q_ref, k_ref, v_ref, hi_ref, lo_ref, full_ref, grad_ref, tab, dq_ref, dk_ref, dv_ref):
    low, up, qd, kd = tab
    zero = jnp.zeros((D, C), BF16)
    for n in range(q_ref.shape[0] // C):
        q, k, v = q_ref[cut(n), :], k_ref[cut(n), :], v_ref[cut(n), :]
        hi, lo = hi_ref[cut(n), :], lo_ref[cut(n), :]
        do = lanes(hi, lo)
        vt = v.T
        sh, sl = split(full_ref[n])
        flat = lanes(vt, sh.T)
        both = nn(do, rows(flat, flat))
        ds = both[:, D:] + nn(hi, sl.T)
        dq = nn(wide(both[:, :D] * low), rows(k, k)) + qd * ds
        dq_ref[cut(n), :] = dq.astype(BF16)
        bh, bl = split(grad_ref[n])
        vb = nn(lanes(v, v), rows(lanes(hi.T, bh.T), lanes(lo.T, bl.T)))
        dk = nn(wide(vb[:, :C] * up), rows(q, q)) + kd * vb[:, C:]
        dk_ref[cut(n), :] = dk.astype(BF16)
        kb = nn(lanes(k, k), lanes(rows(q.T, zero), rows(bh, bl)))
        dv2 = nn(wide(kb[:, :C] * up), rows(do, do))
        dv = dv2[:, :D] + dv2[:, D:] + kd * kb[:, C:]
        dv_ref[cut(n), :] = dv.astype(BF16)


MESH = pl.DeviceIdType.MESH
SMEM = pl.BlockSpec(memory_space=pltpu.SMEM)
ANY = pl.BlockSpec(memory_space=pl.ANY)
TURNS = ((0, 1, 2), (1, 2, 0), (2, 0, 1))
CUTS = ((0, 48), (48, 40), (88, 40))
PARTS = tuple((h, TURNS[h], 0, D) for h in range(3)) + tuple((3, turn, *piece) for turn, piece in zip(TURNS, CUTS))
FINE = PARTS


def flip(place, dim, ring):
    if dim == 0:
        return (place + ring) % (2 * ring)
    if dim == 1:
        return place + 1 - 2 * (place % 2)
    return 2 * ring * (place // ring) + ring - 1 - place


def choose(number, blocks, owners):
    total = None
    for block, owner in zip(blocks, owners):
        part = jnp.where(number == owner, block, 0.0)
        total = part if total is None else total + part
    return total


def main_kernel(
    features, chips, ring,
    dec_hbm, wh_hbm, sz_hbm, gain_hbm, q_hbm, k_hbm, v_hbm, g_hbm, pk_hbm, pv_hbm,
    normed_ref, dq_ref, dk_ref, dv_ref, owned_ref, pk_ref, pv_ref, q_ref, k_ref, v_ref, hi_ref, lo_ref, st_ref, back_ref, tab_ref, pw_ref,
    g_ref, out_ref, sq_ref, cr_ref, sb_ref, cb_ref,
    ag_ref, agsend_ref, agrecv_ref, start_ref, sg_ref, rs1_ref, acc_ref, rs2_ref, rs3_ref,
    dec, wh, sz, gain_ref, qs_ref, gains_ref, tag_ref, tags_ref, msg_ref, all_ref,
    small_sem, in_sem, tag_sem, ag_sem, rs_sem, ar_sem,
):
    rolls, length, width = q_ref.shape
    heads = width // D
    count = length // C
    me = lax.axis_index("roll")
    head_place = lax.axis_index("head")
    chip, core = head_place // 2, head_place % 2
    near = [flip(me, dim, ring) for dim in range(3)]
    others = [((chip + i) % chips) * 2 + side for i in range(chips) for side in (core, 1 - core)][1:]

    loads = []
    for i, (src, dst) in enumerate(((pk_hbm.at[0], pk_ref), (pv_hbm.at[0], pv_ref), (k_hbm, k_ref), (v_hbm, v_ref), (q_hbm, q_ref), (g_hbm, g_ref))):
        loads.append(pltpu.make_async_copy(src, dst, in_sem.at[i]))
    for copy in loads[:2]:
        copy.start()

    smalls = [pltpu.make_async_copy(src, dst, small_sem.at[i]) for i, (src, dst) in enumerate(
        ((dec_hbm, dec), (wh_hbm, wh), (sz_hbm, sz), (gain_hbm, gain_ref)))]
    for copy in smalls:
        copy.start()

    barrier = pltpu.get_barrier_semaphore()
    for place in near:
        pl.semaphore_signal(barrier, inc=1, device_id={"roll": place, "head": head_place}, device_id_type=MESH)
    for place in others:
        pl.semaphore_signal(barrier, inc=1, device_id={"roll": me, "head": place}, device_id_type=MESH)

    def along_roll(src, dst, sems, slot, dim):
        return pltpu.make_async_remote_copy(
            src_ref=src, dst_ref=dst, send_sem=sems.at[0, slot], recv_sem=sems.at[1, slot],
            device_id={"roll": near[dim], "head": head_place}, device_id_type=MESH)

    def along_head(src, dst, sems, slot, place):
        return pltpu.make_async_remote_copy(
            src_ref=src, dst_ref=dst, send_sem=sems.at[0, slot], recv_sem=sems.at[1, slot],
            device_id={"roll": me, "head": place}, device_id_type=MESH)

    for copy in smalls:
        copy.wait()
    line = lax.broadcasted_iota(jnp.int32, (8, D), 0)
    tag_ref[...] = jnp.where(line == 0, wh[0], wh[1])

    for h in range(heads):
        gains_ref[h] = gain_ref[pl.ds(h * D, D)].astype(F32).reshape(1, D)

    def fill(h, _):
        low, up, qd, kd = tables(dec[h])
        tab_ref[h, 0] = low
        tab_ref[h, 1] = up
        tab_ref[h, 2] = qd
        tab_ref[h, 3] = kd
        pw_ref[h] = powers(dec[h], max(count, 2))
        return 0

    lax.fori_loop(0, heads, fill, 0)

    def tab_of(h):
        return tab_ref[h, 0], tab_ref[h, 1], tab_ref[h, 2], tab_ref[h, 3]

    def lane(h):
        return pl.ds(pl.multiple_of(h * D, D), D)

    for copy in loads[:2]:
        copy.wait()
    for copy in loads[2:]:
        copy.start()
    for h in range(heads):
        ag_ref[h, 0] = state_of_prompt(pk_ref.at[:, lane(h)], pv_ref.at[:, lane(h)], tab_ref[h, 3], pw_ref[h])
    pl.semaphore_wait(barrier, 3 + len(others))

    tag_copies = [along_roll(tag_ref, tags_ref.at[dim], tag_sem, dim, dim) for dim in range(3)]
    for copy in tag_copies:
        copy.start()

    def owners_of(order):
        first, second, third = order
        one = flip(me, first, ring)
        return [me, one, flip(me, second, ring), flip(one, second, ring)]

    def gather(i, stage, r=0):
        h, order, low, size = FINE[i]
        cells = pl.ds(low, size)
        src, dst, dim = (
            (ag_ref.at[h, 0, cells], ag_ref.at[h, 1, cells], order[0]),
            (ag_ref.at[h, 0, cells], ag_ref.at[h, 2, cells], order[1]),
            (ag_ref.at[h, 1, cells], ag_ref.at[h, 3, cells], order[1]),
            (agsend_ref.at[h, r, cells], agrecv_ref.at[h, r, cells], order[2]),
        )[stage]
        return along_roll(src, dst, ag_sem, 5 * i + stage + r, dim)

    for stage in range(2):
        for i in range(len(FINE)):
            gather(i, stage).start()

    for copy in loads[2:5]:
        copy.wait()

    def local_unit(u, _):
        h, r = u // rolls, u % rolls
        view = (r, slice(None), lane(h))
        forward_local(q_ref.at[view], k_ref.at[view], v_ref.at[view], tab_of(h), pw_ref[h], out_ref.at[view], st_ref.at[u])
        return 0

    units = heads * rolls
    def parts_of(begin, end):
        return [i for i, part in enumerate(FINE) if begin <= part[0] < end]

    def relay(begin, end):
        for i in parts_of(begin, end):
            gather(i, 0).wait()
            gather(i, 2).start()

    lax.fori_loop(0, 3, local_unit, 0)
    relay(0, 2)
    lax.fori_loop(3, 5, local_unit, 0)
    relay(2, heads)
    lax.fori_loop(5, units, local_unit, 0)
    for copy in tag_copies:
        copy.wait()

    def send_start(i, r):
        h, order, low, size = FINE[i]
        cells = pl.ds(low, size)
        tags = tags_ref[order[2]]
        agsend_ref[h, r, cells] = choose(tags[r:r + 1, :], [ag_ref[h, k, cells] for k in range(4)], owners_of(order))
        gather(i, 3, r).start()

    def take_start(i, r):
        h, order, low, size = FINE[i]
        cells = pl.ds(low, size)
        gather(i, 3, r).wait()
        start_ref[h, r, cells] = agrecv_ref[h, r, cells] + choose(wh[r], [ag_ref[h, k, cells] for k in range(4)], owners_of(order))

    for i in range(len(FINE)):
        gather(i, 1).wait()
        gather(i, 2).wait()
        send_start(i, 0)
    for i in range(len(FINE)):
        send_start(i, 1)
    loads[5].wait()

    def start_units(r, begin, end):
        def unit(h, _):
            view = (r, slice(None), lane(h))
            forward_start(q_ref.at[view], g_ref.at[view], out_ref.at[view], start_ref[h, r], gains_ref[h], sz[r],
                          tab_of(h), pw_ref[h], sq_ref.at[r], cr_ref.at[r], h == 0)
            return 0

        lax.fori_loop(begin, end, unit, 0)

    def pack(total):
        packed = None
        for n in range(count):
            part = jnp.where(line == n, total[:, n * C:(n + 1) * C], 0.0)
            packed = part if packed is None else packed + part
        return packed

    def push(r, i):
        return along_head(msg_ref.at[r], all_ref.at[r, i], ar_sem, len(others) * r + i, others[i])

    def open_sum(r):
        msg_ref[r, 0:8] = pack(row_sums(sq_ref[r]))
        msg_ref[r, 8:16] = pack(row_sums(cr_ref[r]))
        for i in range(len(others)):
            push(r, i).start()

    def close_sum(r):
        for i in range(len(others)):
            push(r, i).wait()
        total = msg_ref[r]
        for i in range(len(others)):
            total = total + all_ref[r, i]
        ss, cross = total[0:8], total[8:16]
        token = line * C + lax.broadcasted_iota(jnp.int32, (8, D), 1)
        scale = jnp.where(token < sz[r], lax.rsqrt(ss / features + EPS), 0.0)
        coef = scale * scale * scale * cross / features
        for n in range(count):
            sb_ref[r, cut(n), :] = column(scale[n:n + 1, :])
            cb_ref[r, cut(n), :] = column(coef[n:n + 1, :])

    def back_units(r, begin, end):
        def unit(h, _):
            view = (r, slice(None), lane(h))
            sg_ref[h, r] = start_back(qs_ref.at[h * rolls + r], g_ref.at[view], out_ref.at[view], sb_ref.at[r], cb_ref.at[r], gains_ref[h], pw_ref[h],
                                      hi_ref.at[view], lo_ref.at[view], back_ref.at[h * rolls + r])
            return 0

        lax.fori_loop(begin, end, unit, 0)

    def scatter(i, stage):
        h, order, low, size = PARTS[i]
        cells = pl.ds(low, size)
        src, dst = (
            (sg_ref.at[h, :, cells], rs1_ref.at[h, :, cells]),
            (acc_ref.at[h, pl.ds(2, 2), cells], rs2_ref.at[h, :, cells]),
            (acc_ref.at[h, pl.ds(1, 1), cells], rs3_ref.at[h, :, cells]),
        )[stage]
        return along_roll(src, dst, rs_sem, 3 * i + stage, order[2 - stage])

    for r in range(rolls):
        for h in range(heads):
            for i in parts_of(h, h + 1):
                take_start(i, r)
            start_units(r, h, h + 1)
        open_sum(r)

    def ready_unit(u, _):
        h, r = u // rolls, u % rolls
        ready(q_ref.at[r, slice(None), lane(h)], st_ref.at[u], qs_ref.at[u], start_ref[h, r], tab_of(h), pw_ref[h])
        return 0

    lax.fori_loop(0, units, ready_unit, 0)
    for r in range(rolls - 1):
        close_sum(r)
        back_units(r, 0, heads)
    close_sum(rolls - 1)
    for h in range(heads):
        back_units(rolls - 1, h, h + 1)
        for i, part in enumerate(PARTS):
            if part[0] == h:
                scatter(i, 0).start()

    def norm_unit(h, r):
        for n in range(count):
            cells = (r, cut(n), lane(h))
            normed_ref[cells] = (out_ref[cells] * sb_ref[r, cut(n), :] * gains_ref[h]).astype(BF16)

    def grad_unit(u, _):
        h, r = u // rolls, u % rolls
        view = (r, slice(None), lane(h))
        backward(q_ref.at[view], k_ref.at[view], v_ref.at[view], hi_ref.at[view], lo_ref.at[view], st_ref.at[u], back_ref.at[u], tab_of(h),
                 dq_ref.at[view], dk_ref.at[view], dv_ref.at[view])
        norm_unit(h, r)
        return 0

    lax.fori_loop(0, 2, grad_unit, 0)
    for i, (h, order, low, size) in enumerate(PARTS):
        cells = pl.ds(low, size)
        tags = tags_ref[order[2]]
        scatter(i, 0).wait()
        for k, owner in enumerate(owners_of(order)):
            total = None
            for r in range(rolls):
                part = jnp.where(wh[r] == owner, sg_ref[h, r, cells], 0.0) + jnp.where(tags[r:r + 1, :] == owner, rs1_ref[h, r, cells], 0.0)
                total = part if total is None else total + part
            acc_ref[h, k, cells] = total
        scatter(i, 1).start()
    lax.fori_loop(2, 5, grad_unit, 0)
    for i, (h, order, low, size) in enumerate(PARTS):
        cells = pl.ds(low, size)
        scatter(i, 1).wait()
        acc_ref[h, 0, cells] += rs2_ref[h, 0, cells]
        acc_ref[h, 1, cells] += rs2_ref[h, 1, cells]
        scatter(i, 2).start()
    lax.fori_loop(5, units - 1, grad_unit, 0)
    norm_unit(heads - 1, rolls - 1)
    for i, (h, order, low, size) in enumerate(PARTS):
        cells = pl.ds(low, size)
        scatter(i, 2).wait()
        owned_ref[h, cells] = acc_ref[h, 0, cells] + rs3_ref[h, 0, cells]


def last_kernel(
    normed, dq, dk, dv, grad, pk, pv, q, k, v, hi, lo, st, back, tab, pw,
    normed_hbm, dq_hbm, dk_hbm, dv_hbm, gk_hbm, gv_hbm, dq_ref, dk_ref, dv_ref, gk_ref, gv_ref, sem,
):
    rolls, length, width = q.shape
    heads = width // D
    h, r = heads - 1, rolls - 1
    copies = []

    def begin(src, dst):
        copy = pltpu.make_async_copy(src, dst, sem.at[len(copies)])
        copy.start()
        copies.append(copy)

    begin(normed, normed_hbm)
    for src, dst in ((dq, dq_hbm), (dk, dk_hbm), (dv, dv_hbm)):
        begin(src.at[pl.ds(0, r)], dst.at[pl.ds(0, r)])
        begin(src.at[r, :, pl.ds(0, h * D)], dst.at[r, :, pl.ds(0, h * D)])

    def unit(h, _):
        view = (slice(None), pl.ds(pl.multiple_of(h * D, D), D))
        prompt_grads(pk.at[view], pv.at[view], grad[h], tab[h, 3], pw[h], gk_ref.at[view], gv_ref.at[view])
        return 0

    lax.fori_loop(0, heads, unit, 0)
    begin(gk_ref, gk_hbm.at[0])
    begin(gv_ref, gv_hbm.at[0])
    view = (r, slice(None), pl.ds(h * D, D))
    u = h * rolls + r
    backward(q.at[view], k.at[view], v.at[view], hi.at[view], lo.at[view], st.at[u], back.at[u], (tab[h, 0], tab[h, 1], tab[h, 2], tab[h, 3]),
             dq_ref, dk_ref, dv_ref)
    for src, dst in ((dq_ref, dq_hbm), (dk_ref, dk_hbm), (dv_ref, dv_hbm)):
        begin(src, dst.at[view])
    for copy in copies:
        copy.wait()


def local(q, k, v, g, pk, pv, which, sizes, decay, gain, features, chips, ring):
    rolls, length, width = q.shape
    heads = width // D
    count = length // C
    units = heads * rolls
    shape = jax.ShapeDtypeStruct
    vmem = pl.BlockSpec(memory_space=pltpu.VMEM)
    tokens = pltpu.VMEM(q.shape, BF16)
    prompt = pltpu.VMEM((length, width), BF16)
    block = lambda *lead: pltpu.VMEM((*lead, D, D), F32)
    dma = lambda *dims: pltpu.SemaphoreType.DMA(dims)
    parts = len(PARTS)
    made = pl.pallas_call(
        functools.partial(main_kernel, features, chips, ring),
        in_specs=[ANY] * 10,
        out_specs=[vmem] * 16,
        out_shape=[tokens] * 4 + [block(heads)] + [prompt] * 2 + [tokens] * 5 + [block(units, count)] * 2 + [block(heads, 4), pltpu.VMEM((heads, max(count, 2), D), F32)],
        scratch_shapes=[tokens, pltpu.VMEM(q.shape, F32)] + [pltpu.VMEM((rolls, length, D), F32)] * 4
        + [block(heads, 4), block(heads, 2), block(heads, 2), block(heads, 2)]
        + [block(heads, 2), block(heads, 2), block(heads, 4), block(heads, 2), block(heads, 1)]
        + [pltpu.SMEM(decay.shape, jnp.int32), pltpu.SMEM(which.shape, jnp.int32), pltpu.SMEM(sizes.shape, jnp.int32), pltpu.VMEM(gain.shape, BF16)]
        + [pltpu.VMEM((units, count, D, 2 * C), BF16), pltpu.VMEM((heads, 1, D), F32), pltpu.VMEM((8, D), jnp.int32), pltpu.VMEM((3, 8, D), jnp.int32)]
        + [pltpu.VMEM((rolls, 16, D), F32), pltpu.VMEM((rolls, 2 * chips - 1, 16, D), F32)]
        + [dma(4), dma(6), dma(2, 3), dma(2, 5 * len(FINE)), dma(2, 3 * parts), dma(2, rolls * (2 * chips - 1))],
        compiler_params=pltpu.CompilerParams(vmem_limit_bytes=26 * 1024 * 1024, collective_id=0, has_side_effects=True),
    )(decay, which, sizes, gain, q, k, v, g, pk, pv)

    return pl.pallas_call(
        last_kernel,
        in_specs=[vmem] * 16,
        out_specs=[ANY] * 6,
        out_shape=[shape(q.shape, BF16)] * 4 + [shape(pk.shape, BF16)] * 2,
        scratch_shapes=[pltpu.VMEM((length, D), BF16)] * 3 + [prompt] * 2 + [dma(12)],
        compiler_params=pltpu.CompilerParams(vmem_limit_bytes=8 * 1024 * 1024),
    )(*made)


def solution(mesh):
    wide_spec = P("roll", None, "head")
    chips = mesh.shape["head"] // 2
    ring = mesh.shape["roll"] // 2

    def run(q, k, v, g, pk, pv, which, sizes, decay, gain):
        body = functools.partial(local, features=gain.shape[0], chips=chips, ring=ring)
        return jax.shard_map(
            body,
            mesh=mesh,
            in_specs=(wide_spec,) * 6 + (P("roll"), P("roll"), P("head"), P("head")),
            out_specs=(wide_spec,) * 6,
            check_vma=False,
        )(q, k, v, g, pk, pv, which, sizes, decay, gain)

    return run
```

```python
import functools

import jax
import jax.numpy as jnp
from jax import lax
from jax.experimental import pallas as pl
from jax.experimental.pallas import tpu as pltpu
from jax.sharding import PartitionSpec as P

F32 = jnp.float32
BF16 = jnp.bfloat16
EPS = 1e-06
D = 128
C = 128


def nn(a, b):
    return lax.dot_general(a, b, (((1,), (0,)), ((), ())), preferred_element_type=F32)


def nt(a, b):
    return lax.dot_general(a, b, (((1,), (1,)), ((), ())), preferred_element_type=F32)


def lanes(a, b):
    return jnp.concatenate([a, b], axis=1)


def rows(a, b):
    return jnp.concatenate([a, b], axis=0)


def split(x):
    hi = x.astype(BF16)
    return hi, (x - hi.astype(F32)).astype(BF16)


def wide(x):
    return lanes(*split(x))


def tall(x):
    return rows(*split(x))


def rate_of(exponent, shape):
    return jnp.exp2(-jnp.full(shape, exponent, jnp.int32).astype(F32))


def tables(exponent):
    rate = rate_of(exponent, (C, C))
    i = lax.broadcasted_iota(jnp.int32, (C, C), 0).astype(F32)
    j = lax.broadcasted_iota(jnp.int32, (C, C), 1).astype(F32)
    gap = i - j
    decay = jnp.exp(-rate * jnp.abs(gap))
    low = jnp.where(gap >= 0.0, decay, 0.0)
    up = jnp.where(gap <= 0.0, decay, 0.0)
    qd = jnp.exp(-rate * (i + 1.0))
    kd = jnp.exp(-rate * (C - 1.0 - i))
    return low, up, qd, kd


def powers(exponent, count):
    return jnp.exp(-rate_of(exponent, (count, D)) * (lax.broadcasted_iota(jnp.int32, (count, D), 0) * C).astype(F32))


def cut(n):
    return pl.ds(n * C, C)


def state_of_prompt(kp, vp, kd, pw):
    count = kp.shape[0] // C
    total = None
    for n in range(count):
        vd = vp[cut(n), :].astype(F32) * (kd * pw[count - 1 - n:count - n])
        kt = kp[cut(n), :].T
        part = nn(lanes(kt, kt), tall(vd))
        total = part if total is None else total + part
    return total


def prompt_grads(kp, vp, grad, kd, pw, gk_ref, gv_ref):
    count = kp.shape[0] // C
    flat, high = wide(grad), tall(grad)
    for n in range(count):
        decay = kd * pw[count - 1 - n:count - n]
        k, v = kp[cut(n), :], vp[cut(n), :]
        gk_ref[cut(n), :] = (nt(lanes(v, v), flat) * decay).astype(BF16)
        gv_ref[cut(n), :] = (nn(lanes(k, k), high) * decay).astype(BF16)


def forward_local(q_ref, k_ref, v_ref, tab, pw, out_ref, state_ref):
    low, up, qd, kd = tab
    step = pw[1:2]
    zero = jnp.zeros((D, C), BF16)
    count = q_ref.shape[0] // C
    state_ref[0] = jnp.zeros((D, D), F32)
    state = None
    for n in range(count - 1):
        kt = k_ref[cut(n), :].T
        part = nn(lanes(kt, kt), tall(v_ref[cut(n), :].astype(F32) * kd))
        state = part if n == 0 else state * step + part
        state_ref[n + 1] = state
    for n in range(count):
        q, k, v = q_ref[cut(n), :], k_ref[cut(n), :], v_ref[cut(n), :]
        kt = k.T
        if n == 0:
            out = nn(wide(nn(q, kt) * low), rows(v, v))
        else:
            both = nn(lanes(q, q), lanes(rows(kt, zero), tall(state_ref[n])))
            out = nn(wide(both[:, :C] * low), rows(v, v)) + qd * both[:, C:]
        out_ref[cut(n), :] = out


def forward_start(q_ref, g_ref, attn_ref, start, gain, size, tab, pw, sq_ref, cr_ref, first):
    low, up, qd, kd = tab
    high = tall(start)
    for n in range(q_ref.shape[0] // C):
        q = q_ref[cut(n), :]
        token = lax.broadcasted_iota(jnp.int32, (C, D), 0) + n * C
        attn = attn_ref[cut(n), :] + nn(lanes(q, q), high) * (qd * pw[n:n + 1])
        attn = jnp.where(token < size, attn, 0.0)
        attn_ref[cut(n), :] = attn
        dyg = g_ref[cut(n), :].astype(F32) * gain
        square, cross = attn * attn, dyg * attn
        sq_ref[cut(n), :] = jnp.where(first, 0.0, sq_ref[cut(n), :]) + square
        cr_ref[cut(n), :] = jnp.where(first, 0.0, cr_ref[cut(n), :]) + cross


def ready(q_ref, state_ref, qs_ref, start, tab, pw):
    low, up, qd, kd = tab
    for n in range(q_ref.shape[0] // C):
        state_ref[n] = state_ref[n] + start * pw[n:n + 1]
        hi, lo = split(q_ref[cut(n), :].astype(F32) * qd)
        qs_ref[n] = lanes(hi.T, lo.T)


def row_sums(x):
    return nt(jnp.ones((8, 2 * D), BF16), wide(x))


def column(row):
    i = lax.broadcasted_iota(jnp.int32, (C, C), 0)
    j = lax.broadcasted_iota(jnp.int32, (C, C), 1)
    spread = jnp.where(i == j, row, 0.0)
    return nn(wide(spread), jnp.ones((2 * C, D), BF16))


def start_back(qs_ref, g_ref, attn_ref, s_ref, c_ref, gain, pw, hi_ref, lo_ref, grad_ref):
    step = pw[1:2]
    total = None
    count = qs_ref.shape[0]
    for n in reversed(range(count)):
        attn = attn_ref[cut(n), :]
        s, c = s_ref[cut(n), :], c_ref[cut(n), :]
        hi, lo = split(s * gain * g_ref[cut(n), :].astype(F32) - c * attn)
        hi_ref[cut(n), :] = hi
        lo_ref[cut(n), :] = lo
        do = lanes(hi, lo)
        both = nn(qs_ref[n], rows(do, do))
        part = both[:, :D] + both[:, D:]
        grad_ref[n] = jnp.zeros((D, D), F32) if total is None else total
        total = part if total is None else total * step + part
    return total


def backward(q_ref, k_ref, v_ref, hi_ref, lo_ref, full_ref, grad_ref, tab, dq_ref, dk_ref, dv_ref):
    low, up, qd, kd = tab
    zero = jnp.zeros((D, C), BF16)
    for n in range(q_ref.shape[0] // C):
        q, k, v = q_ref[cut(n), :], k_ref[cut(n), :], v_ref[cut(n), :]
        hi, lo = hi_ref[cut(n), :], lo_ref[cut(n), :]
        do = lanes(hi, lo)
        vt = v.T
        sh, sl = split(full_ref[n])
        flat = lanes(vt, sh.T)
        both = nn(do, rows(flat, flat))
        ds = both[:, D:] + nn(hi, sl.T)
        dq = nn(wide(both[:, :D] * low), rows(k, k)) + qd * ds
        dq_ref[cut(n), :] = dq.astype(BF16)
        bh, bl = split(grad_ref[n])
        vb = nn(lanes(v, v), rows(lanes(hi.T, bh.T), lanes(lo.T, bl.T)))
        dk = nn(wide(vb[:, :C] * up), rows(q, q)) + kd * vb[:, C:]
        dk_ref[cut(n), :] = dk.astype(BF16)
        kb = nn(lanes(k, k), lanes(rows(q.T, zero), rows(bh, bl)))
        dv2 = nn(wide(kb[:, :C] * up), rows(do, do))
        dv = dv2[:, :D] + dv2[:, D:] + kd * kb[:, C:]
        dv_ref[cut(n), :] = dv.astype(BF16)


MESH = pl.DeviceIdType.MESH
SMEM = pl.BlockSpec(memory_space=pltpu.SMEM)
ANY = pl.BlockSpec(memory_space=pl.ANY)
TURNS = ((0, 1, 2), (1, 2, 0), (2, 0, 1))
CUTS = ((0, 48), (48, 40), (88, 40))
PARTS = tuple((h, TURNS[h], 0, D) for h in range(3)) + tuple((3, turn, *piece) for turn, piece in zip(TURNS, CUTS))
FINE = PARTS


def flip(place, dim, ring):
    if dim == 0:
        return (place + ring) % (2 * ring)
    if dim == 1:
        return place + 1 - 2 * (place % 2)
    return 2 * ring * (place // ring) + ring - 1 - place


def choose(number, blocks, owners):
    total = None
    for block, owner in zip(blocks, owners):
        part = jnp.where(number == owner, block, 0.0)
        total = part if total is None else total + part
    return total


def main_kernel(
    features, chips, ring,
    dec_hbm, wh_hbm, sz_hbm, gain_hbm, q_hbm, k_hbm, v_hbm, g_hbm, pk_hbm, pv_hbm,
    normed_ref, dq_ref, dk_ref, dv_ref, owned_ref, pk_ref, pv_ref, q_ref, k_ref, v_ref, hi_ref, lo_ref, st_ref, back_ref, tab_ref, pw_ref,
    g_ref, out_ref, sq_ref, cr_ref, sb_ref, cb_ref,
    ag_ref, agsend_ref, agrecv_ref, start_ref, sg_ref, rs1_ref, acc_ref, rs2_ref, rs3_ref,
    dec, wh, sz, gain_ref, qs_ref, gains_ref, tag_ref, tags_ref, msg_ref, all_ref,
    small_sem, in_sem, tag_sem, ag_sem, rs_sem, ar_sem,
):
    rolls, length, width = q_ref.shape
    heads = width // D
    count = length // C
    me = lax.axis_index("roll")
    head_place = lax.axis_index("head")
    chip, core = head_place // 2, head_place % 2
    near = [flip(me, dim, ring) for dim in range(3)]
    others = [((chip + i) % chips) * 2 + side for i in range(chips) for side in (core, 1 - core)][1:]

    loads = []
    for i, (src, dst) in enumerate(((pk_hbm.at[0], pk_ref), (pv_hbm.at[0], pv_ref), (k_hbm, k_ref), (v_hbm, v_ref), (q_hbm, q_ref), (g_hbm, g_ref))):
        loads.append(pltpu.make_async_copy(src, dst, in_sem.at[i]))
    for copy in loads[:2]:
        copy.start()

    smalls = [pltpu.make_async_copy(src, dst, small_sem.at[i]) for i, (src, dst) in enumerate(
        ((dec_hbm, dec), (wh_hbm, wh), (sz_hbm, sz), (gain_hbm, gain_ref)))]
    for copy in smalls:
        copy.start()

    barrier = pltpu.get_barrier_semaphore()
    for place in near:
        pl.semaphore_signal(barrier, inc=1, device_id={"roll": place, "head": head_place}, device_id_type=MESH)
    for place in others:
        pl.semaphore_signal(barrier, inc=1, device_id={"roll": me, "head": place}, device_id_type=MESH)

    def along_roll(src, dst, sems, slot, dim):
        return pltpu.make_async_remote_copy(
            src_ref=src, dst_ref=dst, send_sem=sems.at[0, slot], recv_sem=sems.at[1, slot],
            device_id={"roll": near[dim], "head": head_place}, device_id_type=MESH)

    def along_head(src, dst, sems, slot, place):
        return pltpu.make_async_remote_copy(
            src_ref=src, dst_ref=dst, send_sem=sems.at[0, slot], recv_sem=sems.at[1, slot],
            device_id={"roll": me, "head": place}, device_id_type=MESH)

    for copy in smalls:
        copy.wait()
    line = lax.broadcasted_iota(jnp.int32, (8, D), 0)
    tag_ref[...] = jnp.where(line == 0, wh[0], wh[1])

    for h in range(heads):
        gains_ref[h] = gain_ref[pl.ds(h * D, D)].astype(F32).reshape(1, D)

    def fill(h, _):
        low, up, qd, kd = tables(dec[h])
        tab_ref[h, 0] = low
        tab_ref[h, 1] = up
        tab_ref[h, 2] = qd
        tab_ref[h, 3] = kd
        pw_ref[h] = powers(dec[h], max(count, 2))
        return 0

    lax.fori_loop(0, heads, fill, 0)

    def tab_of(h):
        return tab_ref[h, 0], tab_ref[h, 1], tab_ref[h, 2], tab_ref[h, 3]

    def lane(h):
        return pl.ds(pl.multiple_of(h * D, D), D)

    for copy in loads[:2]:
        copy.wait()
    for copy in loads[2:]:
        copy.start()
    def make_state(h):
        ag_ref[h, 0] = state_of_prompt(pk_ref.at[:, lane(h)], pv_ref.at[:, lane(h)], tab_ref[h, 3], pw_ref[h])

    make_state(0)
    pl.semaphore_wait(barrier, 3 + len(others))

    tag_copies = [along_roll(tag_ref, tags_ref.at[dim], tag_sem, dim, dim) for dim in range(3)]
    for copy in tag_copies:
        copy.start()

    def owners_of(order):
        first, second, third = order
        one = flip(me, first, ring)
        return [me, one, flip(me, second, ring), flip(one, second, ring)]

    def gather(i, stage, r=0):
        h, order, low, size = FINE[i]
        cells = pl.ds(low, size)
        src, dst, dim = (
            (ag_ref.at[h, 0, cells], ag_ref.at[h, 1, cells], order[0]),
            (ag_ref.at[h, 0, cells], ag_ref.at[h, 2, cells], order[1]),
            (ag_ref.at[h, 1, cells], ag_ref.at[h, 3, cells], order[1]),
            (agsend_ref.at[h, r, cells], agrecv_ref.at[h, r, cells], order[2]),
        )[stage]
        return along_roll(src, dst, ag_sem, 5 * i + stage + r, dim)

    for h in range(heads):
        if h:
            make_state(h)
        for i, part in enumerate(FINE):
            if part[0] == h:
                gather(i, 0).start()
    for i in range(len(FINE)):
        gather(i, 1).start()

    for copy in loads[2:5]:
        copy.wait()

    def local_unit(u, _):
        h, r = u // rolls, u % rolls
        view = (r, slice(None), lane(h))
        forward_local(q_ref.at[view], k_ref.at[view], v_ref.at[view], tab_of(h), pw_ref[h], out_ref.at[view], st_ref.at[u])
        return 0

    units = heads * rolls
    def parts_of(begin, end):
        return [i for i, part in enumerate(FINE) if begin <= part[0] < end]

    def relay(begin, end):
        for i in parts_of(begin, end):
            gather(i, 0).wait()
            gather(i, 2).start()

    lax.fori_loop(0, 3, local_unit, 0)
    relay(0, 2)
    lax.fori_loop(3, 5, local_unit, 0)
    relay(2, heads)
    lax.fori_loop(5, units, local_unit, 0)
    for copy in tag_copies:
        copy.wait()

    def send_start(i, r):
        h, order, low, size = FINE[i]
        cells = pl.ds(low, size)
        tags = tags_ref[order[2]]
        agsend_ref[h, r, cells] = choose(tags[r:r + 1, :], [ag_ref[h, k, cells] for k in range(4)], owners_of(order))
        gather(i, 3, r).start()

    def take_start(i, r):
        h, order, low, size = FINE[i]
        cells = pl.ds(low, size)
        gather(i, 3, r).wait()
        start_ref[h, r, cells] = agrecv_ref[h, r, cells] + choose(wh[r], [ag_ref[h, k, cells] for k in range(4)], owners_of(order))

    for i in range(len(FINE)):
        gather(i, 1).wait()
        gather(i, 2).wait()
        send_start(i, 0)
    for i in range(len(FINE)):
        send_start(i, 1)
    loads[5].wait()

    def start_units(r, begin, end):
        def unit(h, _):
            view = (r, slice(None), lane(h))
            forward_start(q_ref.at[view], g_ref.at[view], out_ref.at[view], start_ref[h, r], gains_ref[h], sz[r],
                          tab_of(h), pw_ref[h], sq_ref.at[r], cr_ref.at[r], h == 0)
            return 0

        lax.fori_loop(begin, end, unit, 0, unroll=end - begin)

    def pack(total):
        packed = None
        for n in range(count):
            part = jnp.where(line == n, total[:, n * C:(n + 1) * C], 0.0)
            packed = part if packed is None else packed + part
        return packed

    def push(r, i):
        return along_head(msg_ref.at[r], all_ref.at[r, i], ar_sem, len(others) * r + i, others[i])

    def open_sum(r):
        msg_ref[r, 0:8] = pack(row_sums(sq_ref[r]))
        msg_ref[r, 8:16] = pack(row_sums(cr_ref[r]))
        for i in range(len(others)):
            push(r, i).start()

    def close_sum(r):
        for i in range(len(others)):
            push(r, i).wait()
        total = msg_ref[r]
        for i in range(len(others)):
            total = total + all_ref[r, i]
        ss, cross = total[0:8], total[8:16]
        token = line * C + lax.broadcasted_iota(jnp.int32, (8, D), 1)
        scale = jnp.where(token < sz[r], lax.rsqrt(ss / features + EPS), 0.0)
        coef = scale * scale * scale * cross / features
        for n in range(count):
            sb_ref[r, cut(n), :] = column(scale[n:n + 1, :])
            cb_ref[r, cut(n), :] = column(coef[n:n + 1, :])

    def back_units(r, begin, end):
        def unit(h, _):
            view = (r, slice(None), lane(h))
            sg_ref[h, r] = start_back(qs_ref.at[h * rolls + r], g_ref.at[view], out_ref.at[view], sb_ref.at[r], cb_ref.at[r], gains_ref[h], pw_ref[h],
                                      hi_ref.at[view], lo_ref.at[view], back_ref.at[h * rolls + r])
            return 0

        lax.fori_loop(begin, end, unit, 0, unroll=end - begin)

    def scatter(i, stage, r=0):
        h, order, low, size = PARTS[i]
        cells = pl.ds(low, size)
        src, dst = (
            (sg_ref.at[h, r, cells], rs1_ref.at[h, r, cells]),
            (acc_ref.at[h, pl.ds(2, 2), cells], rs2_ref.at[h, :, cells]),
            (acc_ref.at[h, pl.ds(1, 1), cells], rs3_ref.at[h, :, cells]),
        )[stage]
        return along_roll(src, dst, rs_sem, 4 * i + (stage + 1 if stage else r), order[2 - stage])

    for r in range(rolls):
        for begin, end in ((0, 3), (3, heads)):
            for i in parts_of(begin, end):
                take_start(i, r)
            start_units(r, begin, end)
        open_sum(r)

    def ready_unit(u, _):
        h, r = u // rolls, u % rolls
        ready(q_ref.at[r, slice(None), lane(h)], st_ref.at[u], qs_ref.at[u], start_ref[h, r], tab_of(h), pw_ref[h])
        return 0

    lax.fori_loop(0, units, ready_unit, 0)
    for r in range(rolls - 1):
        close_sum(r)
        back_units(r, 0, heads)
        for i in range(len(PARTS)):
            scatter(i, 0, r).start()
    close_sum(rolls - 1)
    for begin, end in ((0, 2), (2, heads)):
        back_units(rolls - 1, begin, end)
        for i, part in enumerate(PARTS):
            if begin <= part[0] < end:
                scatter(i, 0, rolls - 1).start()

    def norm_unit(h, r):
        for n in range(count):
            cells = (r, cut(n), lane(h))
            normed_ref[cells] = (out_ref[cells] * sb_ref[r, cut(n), :] * gains_ref[h]).astype(BF16)

    def grad_unit(u, _):
        h, r = u // rolls, u % rolls
        view = (r, slice(None), lane(h))
        backward(q_ref.at[view], k_ref.at[view], v_ref.at[view], hi_ref.at[view], lo_ref.at[view], st_ref.at[u], back_ref.at[u], tab_of(h),
                 dq_ref.at[view], dk_ref.at[view], dv_ref.at[view])
        norm_unit(h, r)
        return 0

    lax.fori_loop(0, 2, grad_unit, 0, unroll=2)
    for i, (h, order, low, size) in enumerate(PARTS):
        cells = pl.ds(low, size)
        tags = tags_ref[order[2]]
        for r in range(rolls):
            scatter(i, 0, r).wait()
        for k, owner in enumerate(owners_of(order)):
            total = None
            for r in range(rolls):
                part = jnp.where(wh[r] == owner, sg_ref[h, r, cells], 0.0) + jnp.where(tags[r:r + 1, :] == owner, rs1_ref[h, r, cells], 0.0)
                total = part if total is None else total + part
            acc_ref[h, k, cells] = total
        scatter(i, 1).start()
    lax.fori_loop(2, 5, grad_unit, 0, unroll=3)
    for i, (h, order, low, size) in enumerate(PARTS):
        cells = pl.ds(low, size)
        scatter(i, 1).wait()
        acc_ref[h, 0, cells] += rs2_ref[h, 0, cells]
        acc_ref[h, 1, cells] += rs2_ref[h, 1, cells]
        scatter(i, 2).start()
    lax.fori_loop(5, units - 1, grad_unit, 0, unroll=2)
    norm_unit(heads - 1, rolls - 1)
    for i, (h, order, low, size) in enumerate(PARTS):
        cells = pl.ds(low, size)
        scatter(i, 2).wait()
        owned_ref[h, cells] = acc_ref[h, 0, cells] + rs3_ref[h, 0, cells]


def last_kernel(
    normed, dq, dk, dv, grad, pk, pv, q, k, v, hi, lo, st, back, tab, pw,
    normed_hbm, dq_hbm, dk_hbm, dv_hbm, gk_hbm, gv_hbm, dq_ref, dk_ref, dv_ref, gk_ref, gv_ref, sem,
):
    rolls, length, width = q.shape
    heads = width // D
    h, r = heads - 1, rolls - 1
    copies = []

    def begin(src, dst):
        copy = pltpu.make_async_copy(src, dst, sem.at[len(copies)])
        copy.start()
        copies.append(copy)

    begin(normed, normed_hbm)
    for src, dst in ((dq, dq_hbm), (dk, dk_hbm), (dv, dv_hbm)):
        begin(src.at[pl.ds(0, r)], dst.at[pl.ds(0, r)])
        begin(src.at[r, :, pl.ds(0, h * D)], dst.at[r, :, pl.ds(0, h * D)])

    def unit(h, _):
        view = (slice(None), pl.ds(pl.multiple_of(h * D, D), D))
        prompt_grads(pk.at[view], pv.at[view], grad[h], tab[h, 3], pw[h], gk_ref.at[view], gv_ref.at[view])
        return 0

    lax.fori_loop(0, heads, unit, 0, unroll=heads)
    begin(gk_ref, gk_hbm.at[0])
    begin(gv_ref, gv_hbm.at[0])
    view = (r, slice(None), pl.ds(h * D, D))
    u = h * rolls + r
    backward(q.at[view], k.at[view], v.at[view], hi.at[view], lo.at[view], st.at[u], back.at[u], (tab[h, 0], tab[h, 1], tab[h, 2], tab[h, 3]),
             dq_ref, dk_ref, dv_ref)
    for src, dst in ((dq_ref, dq_hbm), (dk_ref, dk_hbm), (dv_ref, dv_hbm)):
        begin(src, dst.at[view])
    for copy in copies:
        copy.wait()


def local(q, k, v, g, pk, pv, which, sizes, decay, gain, features, chips, ring):
    rolls, length, width = q.shape
    heads = width // D
    count = length // C
    units = heads * rolls
    shape = jax.ShapeDtypeStruct
    vmem = pl.BlockSpec(memory_space=pltpu.VMEM)
    tokens = pltpu.VMEM(q.shape, BF16)
    prompt = pltpu.VMEM((length, width), BF16)
    block = lambda *lead: pltpu.VMEM((*lead, D, D), F32)
    dma = lambda *dims: pltpu.SemaphoreType.DMA(dims)
    parts = len(PARTS)
    made = pl.pallas_call(
        functools.partial(main_kernel, features, chips, ring),
        in_specs=[ANY] * 10,
        out_specs=[vmem] * 16,
        out_shape=[tokens] * 4 + [block(heads)] + [prompt] * 2 + [tokens] * 5 + [block(units, count)] * 2 + [block(heads, 4), pltpu.VMEM((heads, max(count, 2), D), F32)],
        scratch_shapes=[tokens, pltpu.VMEM(q.shape, F32)] + [pltpu.VMEM((rolls, length, D), F32)] * 4
        + [block(heads, 4), block(heads, 2), block(heads, 2), block(heads, 2)]
        + [block(heads, 2), block(heads, 2), block(heads, 4), block(heads, 2), block(heads, 1)]
        + [pltpu.SMEM(decay.shape, jnp.int32), pltpu.SMEM(which.shape, jnp.int32), pltpu.SMEM(sizes.shape, jnp.int32), pltpu.VMEM(gain.shape, BF16)]
        + [pltpu.VMEM((units, count, D, 2 * C), BF16), pltpu.VMEM((heads, 1, D), F32), pltpu.VMEM((8, D), jnp.int32), pltpu.VMEM((3, 8, D), jnp.int32)]
        + [pltpu.VMEM((rolls, 16, D), F32), pltpu.VMEM((rolls, 2 * chips - 1, 16, D), F32)]
        + [dma(4), dma(6), dma(2, 3), dma(2, 5 * len(FINE)), dma(2, 4 * parts), dma(2, rolls * (2 * chips - 1))],
        compiler_params=pltpu.CompilerParams(vmem_limit_bytes=26 * 1024 * 1024, collective_id=0, has_side_effects=True),
    )(decay, which, sizes, gain, q, k, v, g, pk, pv)

    return pl.pallas_call(
        last_kernel,
        in_specs=[vmem] * 16,
        out_specs=[ANY] * 6,
        out_shape=[shape(q.shape, BF16)] * 4 + [shape(pk.shape, BF16)] * 2,
        scratch_shapes=[pltpu.VMEM((length, D), BF16)] * 3 + [prompt] * 2 + [dma(12)],
        compiler_params=pltpu.CompilerParams(vmem_limit_bytes=8 * 1024 * 1024),
    )(*made)


def solution(mesh):
    wide_spec = P("roll", None, "head")
    chips = mesh.shape["head"] // 2
    ring = mesh.shape["roll"] // 2

    def run(q, k, v, g, pk, pv, which, sizes, decay, gain):
        body = functools.partial(local, features=gain.shape[0], chips=chips, ring=ring)
        return jax.shard_map(
            body,
            mesh=mesh,
            in_specs=(wide_spec,) * 6 + (P("roll"), P("roll"), P("head"), P("head")),
            out_specs=(wide_spec,) * 6,
            check_vma=False,
        )(q, k, v, g, pk, pv, which, sizes, decay, gain)

    return run
```

```python
import functools

import jax
import jax.numpy as jnp
from jax import lax
from jax.experimental import pallas as pl
from jax.experimental.pallas import tpu as pltpu
from jax.sharding import PartitionSpec as P

F32 = jnp.float32
BF16 = jnp.bfloat16
EPS = 1e-06
D = 128
C = 128


def nn(a, b):
    return lax.dot_general(a, b, (((1,), (0,)), ((), ())), preferred_element_type=F32)


def nt(a, b):
    return lax.dot_general(a, b, (((1,), (1,)), ((), ())), preferred_element_type=F32)


def lanes(a, b):
    return jnp.concatenate([a, b], axis=1)


def rows(a, b):
    return jnp.concatenate([a, b], axis=0)


def split(x):
    hi = x.astype(BF16)
    return hi, (x - hi.astype(F32)).astype(BF16)


def wide(x):
    return lanes(*split(x))


def tall(x):
    return rows(*split(x))


def rate_of(exponent, shape):
    return jnp.exp2(-jnp.full(shape, exponent, jnp.int32).astype(F32))


def tables(exponent):
    rate = rate_of(exponent, (C, C))
    i = lax.broadcasted_iota(jnp.int32, (C, C), 0).astype(F32)
    j = lax.broadcasted_iota(jnp.int32, (C, C), 1).astype(F32)
    gap = i - j
    decay = jnp.exp(-rate * jnp.abs(gap))
    low = jnp.where(gap >= 0.0, decay, 0.0)
    up = jnp.where(gap <= 0.0, decay, 0.0)
    qd = jnp.exp(-rate * (i + 1.0))
    kd = jnp.exp(-rate * (C - 1.0 - i))
    return low, up, qd, kd


def powers(exponent, count):
    return jnp.exp(-rate_of(exponent, (count, D)) * (lax.broadcasted_iota(jnp.int32, (count, D), 0) * C).astype(F32))


def cut(n):
    return pl.ds(n * C, C)


def state_of_prompt(kp, vp, kd, pw):
    count = kp.shape[0] // C
    total = None
    for n in range(count):
        vd = vp[cut(n), :].astype(F32) * (kd * pw[count - 1 - n:count - n])
        kt = kp[cut(n), :].T
        part = nn(lanes(kt, kt), tall(vd))
        total = part if total is None else total + part
    return total


def prompt_grads(kp, vp, grad, kd, pw, gk_ref, gv_ref):
    count = kp.shape[0] // C
    flat, high = wide(grad), tall(grad)
    for n in range(count):
        decay = kd * pw[count - 1 - n:count - n]
        k, v = kp[cut(n), :], vp[cut(n), :]
        gk_ref[cut(n), :] = (nt(lanes(v, v), flat) * decay).astype(BF16)
        gv_ref[cut(n), :] = (nn(lanes(k, k), high) * decay).astype(BF16)


def forward_local(q_ref, k_ref, v_ref, tab, pw, out_ref, state_ref):
    low, up, qd, kd = tab
    step = pw[1:2]
    zero = jnp.zeros((D, C), BF16)
    count = q_ref.shape[0] // C
    state_ref[0] = jnp.zeros((D, D), F32)
    state = None
    for n in range(count - 1):
        kt = k_ref[cut(n), :].T
        part = nn(lanes(kt, kt), tall(v_ref[cut(n), :].astype(F32) * kd))
        state = part if n == 0 else state * step + part
        state_ref[n + 1] = state
    for n in range(count):
        q, k, v = q_ref[cut(n), :], k_ref[cut(n), :], v_ref[cut(n), :]
        kt = k.T
        if n == 0:
            out = nn(wide(nn(q, kt) * low), rows(v, v))
        else:
            both = nn(lanes(q, q), lanes(rows(kt, zero), tall(state_ref[n])))
            out = nn(wide(both[:, :C] * low), rows(v, v)) + qd * both[:, C:]
        out_ref[cut(n), :] = out


def forward_start(q_ref, g_ref, attn_ref, start, gain, size, tab, pw, sq_ref, cr_ref, first):
    low, up, qd, kd = tab
    high = tall(start)
    for n in range(q_ref.shape[0] // C):
        q = q_ref[cut(n), :]
        token = lax.broadcasted_iota(jnp.int32, (C, D), 0) + n * C
        attn = attn_ref[cut(n), :] + nn(lanes(q, q), high) * (qd * pw[n:n + 1])
        attn = jnp.where(token < size, attn, 0.0)
        attn_ref[cut(n), :] = attn
        dyg = g_ref[cut(n), :].astype(F32) * gain
        square, cross = attn * attn, dyg * attn
        sq_ref[cut(n), :] = jnp.where(first, 0.0, sq_ref[cut(n), :]) + square
        cr_ref[cut(n), :] = jnp.where(first, 0.0, cr_ref[cut(n), :]) + cross


def ready(q_ref, state_ref, qs_ref, start, tab, pw):
    low, up, qd, kd = tab
    for n in range(q_ref.shape[0] // C):
        state_ref[n] = state_ref[n] + start * pw[n:n + 1]
        hi, lo = split(q_ref[cut(n), :].astype(F32) * qd)
        qs_ref[n] = lanes(hi.T, lo.T)


def row_sums(x):
    return nt(jnp.ones((8, 2 * D), BF16), wide(x))


def column(row):
    i = lax.broadcasted_iota(jnp.int32, (C, C), 0)
    j = lax.broadcasted_iota(jnp.int32, (C, C), 1)
    spread = jnp.where(i == j, row, 0.0)
    return nn(wide(spread), jnp.ones((2 * C, D), BF16))


def start_back(qs_ref, g_ref, attn_ref, s_ref, c_ref, gain, pw, hi_ref, lo_ref, grad_ref):
    step = pw[1:2]
    total = None
    count = qs_ref.shape[0]
    for n in reversed(range(count)):
        attn = attn_ref[cut(n), :]
        s, c = s_ref[cut(n), :], c_ref[cut(n), :]
        hi, lo = split(s * gain * g_ref[cut(n), :].astype(F32) - c * attn)
        hi_ref[cut(n), :] = hi
        lo_ref[cut(n), :] = lo
        do = lanes(hi, lo)
        both = nn(qs_ref[n], rows(do, do))
        part = both[:, :D] + both[:, D:]
        grad_ref[n] = jnp.zeros((D, D), F32) if total is None else total
        total = part if total is None else total * step + part
    return total


def backward(q_ref, k_ref, v_ref, hi_ref, lo_ref, full_ref, grad_ref, tab, dq_ref, dk_ref, dv_ref):
    low, up, qd, kd = tab
    zero = jnp.zeros((D, C), BF16)
    for n in range(q_ref.shape[0] // C):
        q, k, v = q_ref[cut(n), :], k_ref[cut(n), :], v_ref[cut(n), :]
        hi, lo = hi_ref[cut(n), :], lo_ref[cut(n), :]
        do = lanes(hi, lo)
        vt = v.T
        sh, sl = split(full_ref[n])
        flat = lanes(vt, sh.T)
        both = nn(do, rows(flat, flat))
        ds = both[:, D:] + nn(hi, sl.T)
        dq = nn(wide(both[:, :D] * low), rows(k, k)) + qd * ds
        dq_ref[cut(n), :] = dq.astype(BF16)
        bh, bl = split(grad_ref[n])
        vb = nn(lanes(v, v), rows(lanes(hi.T, bh.T), lanes(lo.T, bl.T)))
        dk = nn(wide(vb[:, :C] * up), rows(q, q)) + kd * vb[:, C:]
        dk_ref[cut(n), :] = dk.astype(BF16)
        kb = nn(lanes(k, k), lanes(rows(q.T, zero), rows(bh, bl)))
        dv2 = nn(wide(kb[:, :C] * up), rows(do, do))
        dv = dv2[:, :D] + dv2[:, D:] + kd * kb[:, C:]
        dv_ref[cut(n), :] = dv.astype(BF16)


MESH = pl.DeviceIdType.MESH
SMEM = pl.BlockSpec(memory_space=pltpu.SMEM)
ANY = pl.BlockSpec(memory_space=pl.ANY)
TURNS = ((0, 1, 2), (1, 2, 0), (2, 0, 1))
CUTS = ((0, 48), (48, 40), (88, 40))
PARTS = tuple((h, TURNS[h], 0, D) for h in range(3)) + tuple((3, turn, *piece) for turn, piece in zip(TURNS, CUTS))
FINE = PARTS


def flip(place, dim, ring):
    if dim == 0:
        return (place + ring) % (2 * ring)
    if dim == 1:
        return place + 1 - 2 * (place % 2)
    return 2 * ring * (place // ring) + ring - 1 - place


def choose(number, blocks, owners):
    total = None
    for block, owner in zip(blocks, owners):
        part = jnp.where(number == owner, block, 0.0)
        total = part if total is None else total + part
    return total


def main_kernel(
    features, chips, ring,
    dec_hbm, wh_hbm, sz_hbm, gain_hbm, q_hbm, k_hbm, v_hbm, g_hbm, pk_hbm, pv_hbm,
    normed_ref, dq_ref, dk_ref, dv_ref, owned_ref, pk_ref, pv_ref, q_ref, k_ref, v_ref, hi_ref, lo_ref, st_ref, back_ref, tab_ref, pw_ref,
    g_ref, out_ref, sq_ref, cr_ref, sb_ref, cb_ref,
    ag_ref, agsend_ref, agrecv_ref, start_ref, sg_ref, rs1_ref, acc_ref, rs2_ref, rs3_ref,
    dec, wh, sz, gain_ref, qs_ref, gains_ref, tag_ref, tags_ref, msg_ref, all_ref,
    small_sem, in_sem, tag_sem, ag_sem, rs_sem, ar_sem,
):
    rolls, length, width = q_ref.shape
    heads = width // D
    count = length // C
    me = lax.axis_index("roll")
    head_place = lax.axis_index("head")
    chip, core = head_place // 2, head_place % 2
    near = [flip(me, dim, ring) for dim in range(3)]
    others = [((chip + i) % chips) * 2 + side for i in range(chips) for side in (core, 1 - core)][1:]

    loads = []
    for i, (src, dst) in enumerate(((pk_hbm.at[0], pk_ref), (pv_hbm.at[0], pv_ref), (k_hbm, k_ref), (v_hbm, v_ref), (q_hbm, q_ref), (g_hbm, g_ref))):
        loads.append(pltpu.make_async_copy(src, dst, in_sem.at[i]))
    for copy in loads[:2]:
        copy.start()

    smalls = [pltpu.make_async_copy(src, dst, small_sem.at[i]) for i, (src, dst) in enumerate(
        ((dec_hbm, dec), (wh_hbm, wh), (sz_hbm, sz), (gain_hbm, gain_ref)))]
    for copy in smalls:
        copy.start()

    barrier = pltpu.get_barrier_semaphore()
    for place in near:
        pl.semaphore_signal(barrier, inc=1, device_id={"roll": place, "head": head_place}, device_id_type=MESH)
    for place in others:
        pl.semaphore_signal(barrier, inc=1, device_id={"roll": me, "head": place}, device_id_type=MESH)

    def along_roll(src, dst, sems, slot, dim):
        return pltpu.make_async_remote_copy(
            src_ref=src, dst_ref=dst, send_sem=sems.at[0, slot], recv_sem=sems.at[1, slot],
            device_id={"roll": near[dim], "head": head_place}, device_id_type=MESH)

    def along_head(src, dst, sems, slot, place):
        return pltpu.make_async_remote_copy(
            src_ref=src, dst_ref=dst, send_sem=sems.at[0, slot], recv_sem=sems.at[1, slot],
            device_id={"roll": me, "head": place}, device_id_type=MESH)

    for copy in smalls:
        copy.wait()
    line = lax.broadcasted_iota(jnp.int32, (8, D), 0)
    tag_ref[...] = jnp.where(line == 0, wh[0], wh[1])

    for h in range(heads):
        gains_ref[h] = gain_ref[pl.ds(h * D, D)].astype(F32).reshape(1, D)

    def fill(h, _):
        low, up, qd, kd = tables(dec[h])
        tab_ref[h, 0] = low
        tab_ref[h, 1] = up
        tab_ref[h, 2] = qd
        tab_ref[h, 3] = kd
        pw_ref[h] = powers(dec[h], max(count, 2))
        return 0

    lax.fori_loop(0, heads, fill, 0)

    def tab_of(h):
        return tab_ref[h, 0], tab_ref[h, 1], tab_ref[h, 2], tab_ref[h, 3]

    def lane(h):
        return pl.ds(pl.multiple_of(h * D, D), D)

    for copy in loads[:2]:
        copy.wait()
    for copy in loads[2:]:
        copy.start()
    def make_state(h):
        ag_ref[h, 0] = state_of_prompt(pk_ref.at[:, lane(h)], pv_ref.at[:, lane(h)], tab_ref[h, 3], pw_ref[h])

    make_state(0)
    pl.semaphore_wait(barrier, 3 + len(others))

    tag_copies = [along_roll(tag_ref, tags_ref.at[dim], tag_sem, dim, dim) for dim in range(3)]
    for copy in tag_copies:
        copy.start()

    def owners_of(order):
        first, second, third = order
        one = flip(me, first, ring)
        return [me, one, flip(me, second, ring), flip(one, second, ring)]

    def gather(i, stage, r=0):
        h, order, low, size = FINE[i]
        cells = pl.ds(low, size)
        src, dst, dim = (
            (ag_ref.at[h, 0, cells], ag_ref.at[h, 1, cells], order[0]),
            (ag_ref.at[h, 0, cells], ag_ref.at[h, 2, cells], order[1]),
            (ag_ref.at[h, 1, cells], ag_ref.at[h, 3, cells], order[1]),
            (agsend_ref.at[h, r, cells], agrecv_ref.at[h, r, cells], order[2]),
        )[stage]
        return along_roll(src, dst, ag_sem, 5 * i + stage + r, dim)

    for h in range(heads):
        if h:
            make_state(h)
        for i, part in enumerate(FINE):
            if part[0] == h:
                gather(i, 0).start()
    for i in range(len(FINE)):
        gather(i, 1).start()

    for copy in loads[2:5]:
        copy.wait()

    def local_unit(u, _):
        h, r = u // rolls, u % rolls
        view = (r, slice(None), lane(h))
        forward_local(q_ref.at[view], k_ref.at[view], v_ref.at[view], tab_of(h), pw_ref[h], out_ref.at[view], st_ref.at[u])
        return 0

    units = heads * rolls
    def parts_of(begin, end):
        return [i for i, part in enumerate(FINE) if begin <= part[0] < end]

    def relay(begin, end):
        for i in parts_of(begin, end):
            gather(i, 0).wait()
            gather(i, 2).start()

    lax.fori_loop(0, 3, local_unit, 0)
    relay(0, 2)
    lax.fori_loop(3, 5, local_unit, 0)
    relay(2, heads)
    lax.fori_loop(5, units, local_unit, 0)
    for copy in tag_copies:
        copy.wait()

    def send_start(i, r):
        h, order, low, size = FINE[i]
        cells = pl.ds(low, size)
        tags = tags_ref[order[2]]
        agsend_ref[h, r, cells] = choose(tags[r:r + 1, :], [ag_ref[h, k, cells] for k in range(4)], owners_of(order))
        gather(i, 3, r).start()

    def take_start(i, r):
        h, order, low, size = FINE[i]
        cells = pl.ds(low, size)
        gather(i, 3, r).wait()
        start_ref[h, r, cells] = agrecv_ref[h, r, cells] + choose(wh[r], [ag_ref[h, k, cells] for k in range(4)], owners_of(order))

    for i in range(len(FINE)):
        gather(i, 1).wait()
        gather(i, 2).wait()
        send_start(i, 0)
    for i in range(len(FINE)):
        send_start(i, 1)
    loads[5].wait()

    def start_units(r, begin, end):
        def unit(h, _):
            view = (r, slice(None), lane(h))
            forward_start(q_ref.at[view], g_ref.at[view], out_ref.at[view], start_ref[h, r], gains_ref[h], sz[r],
                          tab_of(h), pw_ref[h], sq_ref.at[r], cr_ref.at[r], h == 0)
            return 0

        lax.fori_loop(begin, end, unit, 0, unroll=end - begin)

    def pack(total):
        packed = None
        for n in range(count):
            part = jnp.where(line == n, total[:, n * C:(n + 1) * C], 0.0)
            packed = part if packed is None else packed + part
        return packed

    def push(r, i):
        return along_head(msg_ref.at[r], all_ref.at[r, i], ar_sem, len(others) * r + i, others[i])

    def open_sum(r):
        msg_ref[r, 0:8] = pack(row_sums(sq_ref[r]))
        msg_ref[r, 8:16] = pack(row_sums(cr_ref[r]))
        for i in range(len(others)):
            push(r, i).start()

    def close_sum(r):
        for i in range(len(others)):
            push(r, i).wait()
        total = msg_ref[r]
        for i in range(len(others)):
            total = total + all_ref[r, i]
        ss, cross = total[0:8], total[8:16]
        token = line * C + lax.broadcasted_iota(jnp.int32, (8, D), 1)
        scale = jnp.where(token < sz[r], lax.rsqrt(ss / features + EPS), 0.0)
        coef = scale * scale * scale * cross / features
        for n in range(count):
            sb_ref[r, cut(n), :] = column(scale[n:n + 1, :])
            cb_ref[r, cut(n), :] = column(coef[n:n + 1, :])

    def back_units(r, begin, end):
        def unit(h, _):
            view = (r, slice(None), lane(h))
            sg_ref[h, r] = start_back(qs_ref.at[h * rolls + r], g_ref.at[view], out_ref.at[view], sb_ref.at[r], cb_ref.at[r], gains_ref[h], pw_ref[h],
                                      hi_ref.at[view], lo_ref.at[view], back_ref.at[h * rolls + r])
            return 0

        lax.fori_loop(begin, end, unit, 0, unroll=end - begin)

    def scatter(i, stage, r=0):
        h, order, low, size = PARTS[i]
        cells = pl.ds(low, size)
        src, dst = (
            (sg_ref.at[h, r, cells], rs1_ref.at[h, r, cells]),
            (acc_ref.at[h, 2 + r, cells], rs2_ref.at[h, r, cells]),
            (acc_ref.at[h, pl.ds(1, 1), cells], rs3_ref.at[h, :, cells]),
        )[stage]
        return along_roll(src, dst, rs_sem, 5 * i + 2 * stage + r, order[2 - stage])

    for r in range(rolls):
        for begin, end in ((0, 3), (3, heads)):
            for i in parts_of(begin, end):
                take_start(i, r)
            start_units(r, begin, end)
        open_sum(r)

    def ready_unit(u, _):
        h, r = u // rolls, u % rolls
        ready(q_ref.at[r, slice(None), lane(h)], st_ref.at[u], qs_ref.at[u], start_ref[h, r], tab_of(h), pw_ref[h])
        return 0

    lax.fori_loop(0, units, ready_unit, 0)
    for r in range(rolls - 1):
        close_sum(r)
        back_units(r, 0, heads)
        for i in range(len(PARTS)):
            scatter(i, 0, r).start()
    close_sum(rolls - 1)
    for begin, end in ((0, 2), (2, heads)):
        back_units(rolls - 1, begin, end)
        for i, part in enumerate(PARTS):
            if begin <= part[0] < end:
                scatter(i, 0, rolls - 1).start()

    def norm_unit(h, r):
        for n in range(count):
            cells = (r, cut(n), lane(h))
            normed_ref[cells] = (out_ref[cells] * sb_ref[r, cut(n), :] * gains_ref[h]).astype(BF16)

    def grad_unit(u, _):
        h, r = u // rolls, u % rolls
        view = (r, slice(None), lane(h))
        backward(q_ref.at[view], k_ref.at[view], v_ref.at[view], hi_ref.at[view], lo_ref.at[view], st_ref.at[u], back_ref.at[u], tab_of(h),
                 dq_ref.at[view], dk_ref.at[view], dv_ref.at[view])
        norm_unit(h, r)
        return 0

    lax.fori_loop(0, 2, grad_unit, 0, unroll=2)
    for i, (h, order, low, size) in enumerate(PARTS):
        cells = pl.ds(low, size)
        tags = tags_ref[order[2]]
        for r in range(rolls):
            scatter(i, 0, r).wait()
        owners = owners_of(order)
        for k in (3, 2, 1, 0):
            owner, total = owners[k], None
            for r in range(rolls):
                part = jnp.where(wh[r] == owner, sg_ref[h, r, cells], 0.0) + jnp.where(tags[r:r + 1, :] == owner, rs1_ref[h, r, cells], 0.0)
                total = part if total is None else total + part
            acc_ref[h, k, cells] = total
            if k >= 2:
                scatter(i, 1, k - 2).start()
    lax.fori_loop(2, 5, grad_unit, 0, unroll=3)
    for i, (h, order, low, size) in enumerate(PARTS):
        cells = pl.ds(low, size)
        scatter(i, 1, 1).wait()
        acc_ref[h, 1, cells] += rs2_ref[h, 1, cells]
        scatter(i, 2).start()
    lax.fori_loop(5, units - 1, grad_unit, 0, unroll=2)
    norm_unit(heads - 1, rolls - 1)
    for i, (h, order, low, size) in enumerate(PARTS):
        cells = pl.ds(low, size)
        scatter(i, 1, 0).wait()
        scatter(i, 2).wait()
        owned_ref[h, cells] = acc_ref[h, 0, cells] + rs2_ref[h, 0, cells] + rs3_ref[h, 0, cells]


def last_kernel(
    normed, dq, dk, dv, grad, pk, pv, q, k, v, hi, lo, st, back, tab, pw,
    normed_hbm, dq_hbm, dk_hbm, dv_hbm, gk_hbm, gv_hbm, dq_ref, dk_ref, dv_ref, gk_ref, gv_ref, sem,
):
    rolls, length, width = q.shape
    heads = width // D
    h, r = heads - 1, rolls - 1
    copies = []

    def begin(src, dst):
        copy = pltpu.make_async_copy(src, dst, sem.at[len(copies)])
        copy.start()
        copies.append(copy)

    begin(normed, normed_hbm)
    for src, dst in ((dq, dq_hbm), (dk, dk_hbm), (dv, dv_hbm)):
        begin(src.at[pl.ds(0, r)], dst.at[pl.ds(0, r)])
        begin(src.at[r, :, pl.ds(0, h * D)], dst.at[r, :, pl.ds(0, h * D)])

    def unit(h, _):
        view = (slice(None), pl.ds(pl.multiple_of(h * D, D), D))
        prompt_grads(pk.at[view], pv.at[view], grad[h], tab[h, 3], pw[h], gk_ref.at[view], gv_ref.at[view])
        return 0

    lax.fori_loop(0, heads, unit, 0)
    begin(gk_ref, gk_hbm.at[0])
    begin(gv_ref, gv_hbm.at[0])
    u = h * rolls + r
    half, blocks = length // 2, st.shape[1] // 2
    table = tab[h, 0], tab[h, 1], tab[h, 2], tab[h, 3]

    def side(i, _):
        cells = pl.ds(pl.multiple_of(i * half, half), half)
        view = (r, cells, pl.ds(h * D, D))
        part = (u, pl.ds(i * blocks, blocks))
        backward(q.at[view], k.at[view], v.at[view], hi.at[view], lo.at[view], st.at[part], back.at[part], table,
                 dq_ref.at[cells], dk_ref.at[cells], dv_ref.at[cells])
        return 0

    lax.fori_loop(0, 2, side, 0)
    view = (r, slice(None), pl.ds(h * D, D))
    for src, dst in ((dq_ref, dq_hbm), (dk_ref, dk_hbm), (dv_ref, dv_hbm)):
        begin(src, dst.at[view])
    for copy in copies:
        copy.wait()


def local(q, k, v, g, pk, pv, which, sizes, decay, gain, features, chips, ring):
    rolls, length, width = q.shape
    heads = width // D
    count = length // C
    units = heads * rolls
    shape = jax.ShapeDtypeStruct
    vmem = pl.BlockSpec(memory_space=pltpu.VMEM)
    tokens = pltpu.VMEM(q.shape, BF16)
    prompt = pltpu.VMEM((length, width), BF16)
    block = lambda *lead: pltpu.VMEM((*lead, D, D), F32)
    dma = lambda *dims: pltpu.SemaphoreType.DMA(dims)
    parts = len(PARTS)
    made = pl.pallas_call(
        functools.partial(main_kernel, features, chips, ring),
        in_specs=[ANY] * 10,
        out_specs=[vmem] * 16,
        out_shape=[tokens] * 4 + [block(heads)] + [prompt] * 2 + [tokens] * 5 + [block(units, count)] * 2 + [block(heads, 4), pltpu.VMEM((heads, max(count, 2), D), F32)],
        scratch_shapes=[tokens, pltpu.VMEM(q.shape, F32)] + [pltpu.VMEM((rolls, length, D), F32)] * 4
        + [block(heads, 4), block(heads, 2), block(heads, 2), block(heads, 2)]
        + [block(heads, 2), block(heads, 2), block(heads, 4), block(heads, 2), block(heads, 1)]
        + [pltpu.SMEM(decay.shape, jnp.int32), pltpu.SMEM(which.shape, jnp.int32), pltpu.SMEM(sizes.shape, jnp.int32), pltpu.VMEM(gain.shape, BF16)]
        + [pltpu.VMEM((units, count, D, 2 * C), BF16), pltpu.VMEM((heads, 1, D), F32), pltpu.VMEM((8, D), jnp.int32), pltpu.VMEM((3, 8, D), jnp.int32)]
        + [pltpu.VMEM((rolls, 16, D), F32), pltpu.VMEM((rolls, 2 * chips - 1, 16, D), F32)]
        + [dma(4), dma(6), dma(2, 3), dma(2, 5 * len(FINE)), dma(2, 5 * parts), dma(2, rolls * (2 * chips - 1))],
        compiler_params=pltpu.CompilerParams(vmem_limit_bytes=26 * 1024 * 1024, collective_id=0, has_side_effects=True),
    )(decay, which, sizes, gain, q, k, v, g, pk, pv)

    return pl.pallas_call(
        last_kernel,
        in_specs=[vmem] * 16,
        out_specs=[ANY] * 6,
        out_shape=[shape(q.shape, BF16)] * 4 + [shape(pk.shape, BF16)] * 2,
        scratch_shapes=[pltpu.VMEM((length, D), BF16)] * 3 + [prompt] * 2 + [dma(12)],
        compiler_params=pltpu.CompilerParams(vmem_limit_bytes=8 * 1024 * 1024),
    )(*made)


def solution(mesh):
    wide_spec = P("roll", None, "head")
    chips = mesh.shape["head"] // 2
    ring = mesh.shape["roll"] // 2

    def run(q, k, v, g, pk, pv, which, sizes, decay, gain):
        body = functools.partial(local, features=gain.shape[0], chips=chips, ring=ring)
        return jax.shard_map(
            body,
            mesh=mesh,
            in_specs=(wide_spec,) * 6 + (P("roll"), P("roll"), P("head"), P("head")),
            out_specs=(wide_spec,) * 6,
            check_vma=False,
        )(q, k, v, g, pk, pv, which, sizes, decay, gain)

    return run
```
